512 devices in a mesh: dom: 32 (over z, core), feat: 16 (over x, y).
Axes of the slice: x: 4, y: 4, z: 16, core: 2. Of those that a mesh axis runs over, the one named last changes fastest.
Arguments:
- grad_out: bfloat16 [512, 24576], P('feat', 'dom'), may hold values from -6 to 6
- saved_agg: bfloat16 [512, 24576], P('feat', 'dom'), may hold values from -0.09375 to 0.09375
- weight: bfloat16 [512, 512], P('feat'), may hold values from -0.25 to 0.25
- tile_values: bfloat16 [3072, 128, 128], P('dom'), may hold values from 0 to 0.029907227
- tile_dst: int32 [3072], P('dom'), may hold values from 0 to 5
- tile_slot: int32 [3072], P('dom'), may hold values from 0 to 31
- tile_count: int32 [32], P('dom'), may hold values from 12 to 96, as said below
- mirror_owner: int32 [32, 32], P('dom'), may hold values from 0 to 31, each once within a row
- mirror_local: int32 [32, 32], P('dom'), may hold values from 0 to 5
Outputs:
- grad_nodes: bfloat16 [512, 24576], P('feat', 'dom')
- grad_mirrors: bfloat16 [512, 131072], P('feat', 'dom')
- weight_grad: float32 [512, 512], P('feat')
The draws below stay inside these ranges and needn't reach their ends.
Inputs may be any that keep to these rules, and one draw needn't show every extreme that they name: Every partition's first tile_count tiles are live, the rest are padding; some partition has all 96 live in every draw. `mirror_owner`: each partition's row names every partition once.
All inputs are finite; a program needn't handle non-finite values.
Results may differ from the reference program's by a relative error of at most 0.0049.
Values may be sent and summed in bfloat16 or wider, within the bound.
No kernel may reach another device: no remote copies, remote signals or barrier semaphores. Data moves between devices by JAX's collectives and lax.ppermute only.
A program may use at most 64 MiB of HBM per device.

```python
import jax
import jax.numpy as jnp
from jax import lax

H = 512
TILE = 128
VB_DEV = 6
TILES_DEV = 96
NODES = 24576
TILES = 3072
N_DOM = 32


def draw_tile_count(key, part):
    key = jax.random.fold_in(key, 7)
    first_key, second_key = jax.random.split(key)
    lowest = max(1, TILES_DEV // 8)
    counts = jax.random.randint(first_key, (N_DOM,), lowest, TILES_DEV + 1)
    fullest = jax.random.randint(second_key, (), 0, N_DOM)
    return counts.at[fullest].set(TILES_DEV).astype(jnp.int32)


def touch_ends(array, own_key, least, largest):
    extent = array.shape
    place = [jax.random.randint(jax.random.fold_in(own_key, axis), (), 0, extent[axis]) for axis in range(len(extent))]
    array = array.at[tuple(place)].set(least)
    longest = extent.index(max(extent))
    place[longest] = (place[longest] + 1) % extent[longest]
    return array.at[tuple(place)].set(largest)


def block_levels(stream_key, dims, cuts, smallest, high):
    factor_of = 1.0
    for position, blocks in cuts:
        heights = jax.random.uniform(jax.random.fold_in(jax.random.fold_in(stream_key, 6), position), (blocks,), jnp.float32, smallest / len(cuts), high / len(cuts))
        factor_of = factor_of * jnp.repeat(jnp.exp(heights), dims[position] // blocks).reshape((-1,) + (1,) * (len(dims) - 1 - position))
    return factor_of


def centred(stream_key, shape, width, most, shards=(), held_as=jnp.bfloat16):
    factor_of = block_levels(stream_key, shape, shards, -0.22, 0.18) if shards else 1.0
    values = jax.random.normal(stream_key, shape, jnp.float32) * width * factor_of
    return jnp.minimum(jnp.maximum(values, -most), most).astype(held_as)


def setup_inputs(seed: int = 0) -> dict:
    key_of = jax.random.split(jax.random.key(seed), 10)
    return {
        "grad_out": centred(key_of[0], (H, NODES), 1.0, 6.0, ((0, 16), (1, 32))),
        "saved_agg": centred(key_of[1], (H, NODES), (1.0 / NODES ** 0.5), 0.09375, ((0, 16), (1, 32))),
        "weight": centred(key_of[2], (H, H), H ** -0.5, 0.25, ((0, 16),)),
        "tile_values": jnp.clip(0.029907227 * jax.random.uniform(key_of[3], (TILES, TILE, TILE), jnp.float32) ** block_levels(key_of[3], (TILES, TILE, TILE), ((0, 32),), -0.2, 0.2), 0.0, 0.029907227).astype(jnp.bfloat16),
        "tile_dst": touch_ends(jax.random.randint(key_of[4], (TILES,), 0, VB_DEV), jax.random.fold_in(key_of[4], 1), 0, VB_DEV - 1).astype(jnp.int32),
        "tile_slot": touch_ends(jax.random.randint(key_of[5], (TILES,), 0, N_DOM), jax.random.fold_in(key_of[5], 1), 0, N_DOM - 1).astype(jnp.int32),
        "tile_count": draw_tile_count(jax.random.fold_in(key_of[9], 71), 0),
        "mirror_owner": jax.vmap(lambda own: jax.random.permutation(own, N_DOM))(jax.random.split(key_of[7], N_DOM)).reshape((N_DOM, N_DOM)).astype(jnp.int32),
        "mirror_local": touch_ends(jax.random.randint(key_of[8], (N_DOM, N_DOM), 0, VB_DEV), jax.random.fold_in(key_of[8], 1), 0, VB_DEV - 1).astype(jnp.int32),
    }


def reference(grad_out, saved_agg, weight, tile_values, tile_dst, tile_slot, tile_count, mirror_owner, mirror_local):
    weight_grad = jnp.dot(saved_agg, grad_out.T, preferred_element_type=jnp.float32)
    back_sum = jnp.dot(weight, grad_out, preferred_element_type=jnp.float32).astype(jnp.bfloat16)
    block_total = N_DOM * VB_DEV
    spread = back_sum.reshape(H, block_total, TILE)

    def per_device(carry, device):
        start = device * TILES_DEV
        values = lax.dynamic_slice_in_dim(tile_values, start, TILES_DEV, 0)
        dst_block = lax.dynamic_slice_in_dim(tile_dst, start, TILES_DEV, 0) + device * VB_DEV
        slot_index = lax.dynamic_slice_in_dim(tile_slot, start, TILES_DEV, 0)
        owners = jnp.take(mirror_owner[device], slot_index)
        locals_row = jnp.take(mirror_local[device], slot_index)
        target = (owners * VB_DEV + locals_row).astype(jnp.int32)
        sources = jnp.take(spread, dst_block.astype(jnp.int32), axis=1).astype(jnp.float32)
        products = jnp.einsum("ftk,tkj->tfj", sources, values.astype(jnp.float32))
        live_tiles = (jnp.arange(TILES_DEV, dtype=jnp.int32) < tile_count[device]).astype(jnp.float32)
        products = products * live_tiles[:, None, None]
        return carry.at[target].add(products), None

    start_carry = jnp.zeros((block_total, H, TILE), jnp.float32)
    summed = lax.scan(per_device, start_carry, jnp.arange(N_DOM, dtype=jnp.int32))[0]
    grad_nodes = summed.transpose(1, 0, 2).reshape(H, block_total * TILE).astype(jnp.bfloat16)
    mirror_target = (mirror_owner * VB_DEV + mirror_local).reshape(-1).astype(jnp.int32)
    grad_mirrors = jnp.take(grad_nodes.reshape(H, block_total, TILE), mirror_target, axis=1)
    grad_mirrors = grad_mirrors.reshape(H, N_DOM * N_DOM * TILE)
    return grad_nodes, grad_mirrors, weight_grad
```

```python
import functools

import jax
import jax.numpy as jnp
from jax import lax
from jax.experimental import pallas as pl
from jax.experimental.pallas import tpu as pltpu
from jax.sharding import PartitionSpec as P

LANES = 128
UNROLL = 8
EXTRA = 8
VMEM_BYTES = 16 * 1024 * 1024


def partial_kernel(
    dst_ref, slot_ref, count_ref, owner_ref, local_ref,
    piece_ref, weight_ref, agg_ref, tiles_ref,
    msg_ref,
    back_ref, acc_ref, extra_ref,
):
    block_count, rows, _ = back_ref.shape
    peers = msg_ref.shape[0]
    tile_total = tiles_ref.shape[0]
    wide = weight_ref.shape[1] // LANES
    piece = piece_ref[...]
    back = jnp.dot(weight_ref[...], piece, preferred_element_type=jnp.float32)
    back = back.astype(jnp.bfloat16)
    for b in range(block_count):
        back_ref[b] = back[:, b * LANES : (b + 1) * LANES]
    acc_ref[...] = jnp.zeros_like(acc_ref)
    count = count_ref[0]

    def step(i, carry):
        products, places = [], []
        for u in range(UNROLL):
            t = i * UNROLL + u
            products.append(
                jnp.dot(back_ref[dst_ref[t]], tiles_ref[t], preferred_element_type=jnp.float32)
            )
            places.append(jnp.where(t < count, owner_ref[0, slot_ref[t]], peers))
        for place, product in zip(places, products):
            acc_ref[place] += product
        return carry

    lax.fori_loop(0, tile_total // UNROLL, step, 0)

    term = lax.dot_general(
        agg_ref[...], piece, (((1,), (1,)), ((), ())), preferred_element_type=jnp.float32
    )
    for k in range(wide):
        extra_ref[:, k, :] = term[:, k * LANES : (k + 1) * LANES]
    for k in range(wide, EXTRA):
        extra_ref[:, k, :] = jnp.zeros((peers, LANES), jnp.float32)

    def number(s, carry):
        value = local_ref[0, s].astype(jnp.float32)
        extra_ref[owner_ref[0, s], pl.ds(wide, 1), :] = jnp.full((1, LANES), value, jnp.float32)
        return carry

    lax.fori_loop(0, peers, number, 0)
    msg_ref[:, :rows, :] = acc_ref[:peers].astype(jnp.bfloat16)
    msg_ref[:, rows:, :] = extra_ref[...].astype(jnp.bfloat16)


def master_kernel(wide, got_ref, nodes_ref, msg_ref):
    peers, height, _ = got_ref.shape
    rows, columns = nodes_ref.shape
    block_count = columns // LANES
    tail = got_ref[:, rows:, :].astype(jnp.float32)
    numbers = [tail[p, wide : wide + 1, :] for p in range(peers)]
    sums = [jnp.zeros((rows, LANES), jnp.float32) for _ in range(block_count)]
    for p in range(peers):
        part = got_ref[p, :rows, :].astype(jnp.float32)
        for b in range(block_count):
            sums[b] = sums[b] + jnp.where(numbers[p] == float(b), part, 0.0)
    for b in range(block_count):
        nodes_ref[:, b * LANES : (b + 1) * LANES] = sums[b].astype(jnp.bfloat16)
    for p in range(peers):
        pick = sums[0]
        for b in range(1, block_count):
            pick = jnp.where(numbers[p] == float(b), sums[b], pick)
        msg_ref[p, :rows, :] = pick.astype(jnp.bfloat16)
    total = jnp.sum(tail, axis=0)
    high = total[:wide].astype(jnp.bfloat16)
    low = (total[:wide] - high.astype(jnp.float32)).astype(jnp.bfloat16)
    both = jnp.concatenate([high.astype(jnp.float32), low.astype(jnp.float32)], axis=0)
    both = both.astype(jnp.bfloat16)
    for p in range(peers):
        msg_ref[p, rows:, :] = both


def mirror_kernel(wide, owner_ref, got_ref, mirrors_ref, wgrad_ref):
    peers = got_ref.shape[0]
    rows = mirrors_ref.shape[0]
    for s in range(peers):
        mirrors_ref[:, s * LANES : (s + 1) * LANES] = got_ref[owner_ref[0, s], :rows, :]
    tail = got_ref[:, rows:, :].astype(jnp.float32)
    for k in range(wide):
        wgrad_ref[:, k * LANES : (k + 1) * LANES] = tail[:, k, :] + tail[:, wide + k, :]


def body(
    grad_out,
    saved_agg,
    weight,
    tile_values,
    tile_dst,
    tile_slot,
    tile_count,
    mirror_owner,
    mirror_local,
):
    rows, columns = grad_out.shape
    block_count = columns // LANES
    peers = mirror_owner.shape[1]
    features = weight.shape[1]
    wide = features // LANES
    groups = features // rows
    height = rows + EXTRA
    vmem = pl.BlockSpec(memory_space=pltpu.VMEM)
    smem = pl.BlockSpec(memory_space=pltpu.SMEM)
    params = pltpu.CompilerParams(vmem_limit_bytes=VMEM_BYTES)

    with jax.named_scope("gather_features"):
        copies = jnp.broadcast_to(grad_out[None], (groups, rows, columns))
        piece = lax.all_to_all(copies, "feat", 0, 0, tiled=True).reshape(features, columns)
    message = pl.pallas_call(
        partial_kernel,
        out_shape=jax.ShapeDtypeStruct((peers, height, LANES), jnp.bfloat16),
        in_specs=[smem] * 5 + [vmem] * 4,
        out_specs=vmem,
        scratch_shapes=[
            pltpu.VMEM((block_count, rows, LANES), jnp.bfloat16),
            pltpu.VMEM((peers + 1, rows, LANES), jnp.float32),
            pltpu.VMEM((peers, EXTRA, LANES), jnp.float32),
        ],
        compiler_params=params,
        name="partials",
    )(
        tile_dst, tile_slot, tile_count, mirror_owner, mirror_local,
        piece, weight, saved_agg, tile_values,
    )
    with jax.named_scope("to_masters"):
        got = lax.all_to_all(message, "dom", 0, 0, tiled=True)
    grad_nodes, answer = pl.pallas_call(
        functools.partial(master_kernel, wide),
        out_shape=(
            jax.ShapeDtypeStruct((rows, columns), jnp.bfloat16),
            jax.ShapeDtypeStruct((peers, height, LANES), jnp.bfloat16),
        ),
        in_specs=[vmem],
        out_specs=(vmem, vmem),
        compiler_params=params,
        name="masters",
    )(got)
    with jax.named_scope("to_mirrors"):
        back = lax.all_to_all(answer, "dom", 0, 0, tiled=True)
    grad_mirrors, weight_grad = pl.pallas_call(
        functools.partial(mirror_kernel, wide),
        out_shape=(
            jax.ShapeDtypeStruct((rows, peers * LANES), jnp.bfloat16),
            jax.ShapeDtypeStruct((rows, features), jnp.float32),
        ),
        in_specs=[smem, vmem],
        out_specs=(vmem, vmem),
        compiler_params=params,
        name="mirrors",
    )(mirror_owner, back)
    return (grad_nodes, grad_mirrors, weight_grad)


def solution(mesh):
    in_specs = (
        P("feat", "dom"),
        P("feat", "dom"),
        P("feat", None),
        P("dom", None, None),
        P("dom"),
        P("dom"),
        P("dom"),
        P("dom", None),
        P("dom", None),
    )
    out_specs = (P("feat", "dom"), P("feat", "dom"), P("feat", None))
    return jax.shard_map(body, mesh=mesh, in_specs=in_specs, out_specs=out_specs, check_vma=False)
```

```python
import functools

import jax
import jax.numpy as jnp
from jax import lax
from jax.experimental import pallas as pl
from jax.experimental.pallas import tpu as pltpu
from jax.sharding import PartitionSpec as P

LANES = 128
UNROLL = 8
EXTRA = 8
TILE_PARTS = 4
VMEM_BYTES = 16 * 1024 * 1024


def spread_kernel(source_ref, copies_ref, sems):
    count = copies_ref.shape[0]
    moves = [
        pltpu.make_async_copy(source_ref, copies_ref.at[k], sems.at[k]) for k in range(count)
    ]
    for move in moves:
        move.start()
    for move in moves:
        move.wait()


def partial_kernel(
    dst_hbm, slot_hbm, count_ref, owner_hbm, local_hbm,
    piece_ref, weight_hbm, agg_hbm, tiles_hbm,
    msg_ref,
    dst_ref, slot_ref, owner_ref, local_ref, weight_ref, agg_ref, tiles_ref,
    back_ref, acc_ref, extra_ref, sems,
):
    block_count, rows, _ = back_ref.shape
    peers = msg_ref.shape[0]
    tile_total = tiles_ref.shape[0]
    wide = weight_ref.shape[1] // LANES
    pairs = [
        (weight_hbm, weight_ref), (dst_hbm, dst_ref), (slot_hbm, slot_ref),
        (owner_hbm, owner_ref), (local_hbm, local_ref), (agg_hbm, agg_ref),
    ]
    part = tile_total // TILE_PARTS
    for k in range(TILE_PARTS):
        pairs.append((tiles_hbm.at[pl.ds(k * part, part)], tiles_ref.at[pl.ds(k * part, part)]))
    moves = [pltpu.make_async_copy(a, b, sems.at[k]) for k, (a, b) in enumerate(pairs)]
    for move in moves:
        move.start()
    acc_ref[...] = jnp.zeros_like(acc_ref)
    piece = piece_ref[...]
    moves[0].wait()
    back = jnp.dot(weight_ref[...], piece, preferred_element_type=jnp.float32)
    back = back.astype(jnp.bfloat16)
    for b in range(block_count):
        back_ref[b] = back[:, b * LANES : (b + 1) * LANES]
    for move in moves[1:6]:
        move.wait()
    term = lax.dot_general(
        agg_ref[...], piece, (((1,), (1,)), ((), ())), preferred_element_type=jnp.float32
    )
    for k in range(wide):
        extra_ref[:, k, :] = term[:, k * LANES : (k + 1) * LANES]
    for k in range(wide, EXTRA):
        extra_ref[:, k, :] = jnp.zeros((peers, LANES), jnp.float32)

    def number(s, carry):
        value = local_ref[0, s].astype(jnp.float32)
        extra_ref[owner_ref[0, s], pl.ds(wide, 1), :] = jnp.full((1, LANES), value, jnp.float32)
        return carry

    lax.fori_loop(0, peers, number, 0)
    msg_ref[:, rows:, :] = extra_ref[...].astype(jnp.bfloat16)
    count = count_ref[0]

    def step(i, carry):
        products, places = [], []
        for u in range(UNROLL):
            t = i * UNROLL + u
            products.append(
                jnp.dot(back_ref[dst_ref[t]], tiles_ref[t], preferred_element_type=jnp.float32)
            )
            places.append(jnp.where(t < count, owner_ref[0, slot_ref[t]], peers))
        for place, product in zip(places, products):
            acc_ref[place] += product
        return carry

    for k in range(TILE_PARTS):
        moves[6 + k].wait()
        lax.fori_loop(k * part // UNROLL, (k + 1) * part // UNROLL, step, 0)
    msg_ref[:, :rows, :] = acc_ref[:peers].astype(jnp.bfloat16)


def master_kernel(wide, got_ref, nodes_ref, msg_ref):
    peers, height, _ = got_ref.shape
    rows, columns = nodes_ref.shape
    block_count = columns // LANES
    tail = got_ref[:, rows:, :].astype(jnp.float32)
    numbers = [tail[p, wide : wide + 1, :] for p in range(peers)]
    sums = [jnp.zeros((rows, LANES), jnp.float32) for _ in range(block_count)]
    for p in range(peers):
        part = got_ref[p, :rows, :].astype(jnp.float32)
        for b in range(block_count):
            sums[b] = sums[b] + jnp.where(numbers[p] == float(b), part, 0.0)
    for b in range(block_count):
        nodes_ref[:, b * LANES : (b + 1) * LANES] = sums[b].astype(jnp.bfloat16)
    for p in range(peers):
        pick = sums[0]
        for b in range(1, block_count):
            pick = jnp.where(numbers[p] == float(b), sums[b], pick)
        msg_ref[p, :rows, :] = pick.astype(jnp.bfloat16)
    total = jnp.sum(tail, axis=0)
    high = total[:wide].astype(jnp.bfloat16)
    low = (total[:wide] - high.astype(jnp.float32)).astype(jnp.bfloat16)
    both = jnp.concatenate([high.astype(jnp.float32), low.astype(jnp.float32)], axis=0)
    both = both.astype(jnp.bfloat16)
    for p in range(peers):
        msg_ref[p, rows:, :] = both


def mirror_kernel(wide, owner_ref, got_ref, mirrors_ref, wgrad_ref):
    peers = got_ref.shape[0]
    rows = mirrors_ref.shape[0]
    for s in range(peers):
        mirrors_ref[:, s * LANES : (s + 1) * LANES] = got_ref[owner_ref[0, s], :rows, :]
    tail = got_ref[:, rows:, :].astype(jnp.float32)
    for k in range(wide):
        wgrad_ref[:, k * LANES : (k + 1) * LANES] = tail[:, k, :] + tail[:, wide + k, :]


def in_hbm(array):
    return pltpu.with_memory_space_constraint(array, pltpu.HBM)


def body(
    grad_out,
    saved_agg,
    weight,
    tile_values,
    tile_dst,
    tile_slot,
    tile_count,
    mirror_owner,
    mirror_local,
):
    rows, columns = grad_out.shape
    block_count = columns // LANES
    peers = mirror_owner.shape[1]
    features = weight.shape[1]
    wide = features // LANES
    groups = features // rows
    height = rows + EXTRA
    vmem = pl.BlockSpec(memory_space=pltpu.VMEM)
    smem = pl.BlockSpec(memory_space=pltpu.SMEM)
    hbm = pl.BlockSpec(memory_space=pltpu.HBM)
    params = pltpu.CompilerParams(vmem_limit_bytes=VMEM_BYTES)

    copies = pl.pallas_call(
        spread_kernel,
        out_shape=jax.ShapeDtypeStruct((groups, rows, columns), grad_out.dtype),
        in_specs=[hbm],
        out_specs=vmem,
        scratch_shapes=[pltpu.SemaphoreType.DMA((groups,))],
        compiler_params=params,
        name="spread",
    )(in_hbm(grad_out))
    with jax.named_scope("gather_features"):
        piece = lax.all_to_all(copies, "feat", 0, 0, tiled=True).reshape(features, columns)
    message = pl.pallas_call(
        partial_kernel,
        out_shape=jax.ShapeDtypeStruct((peers, height, LANES), jnp.bfloat16),
        in_specs=[hbm] * 2 + [smem] + [hbm] * 2 + [vmem] + [hbm] * 3,
        out_specs=vmem,
        scratch_shapes=[
            pltpu.SMEM(tile_dst.shape, jnp.int32),
            pltpu.SMEM(tile_slot.shape, jnp.int32),
            pltpu.SMEM(mirror_owner.shape, jnp.int32),
            pltpu.SMEM(mirror_local.shape, jnp.int32),
            pltpu.VMEM(weight.shape, jnp.bfloat16),
            pltpu.VMEM(saved_agg.shape, jnp.bfloat16),
            pltpu.VMEM(tile_values.shape, jnp.bfloat16),
            pltpu.VMEM((block_count, rows, LANES), jnp.bfloat16),
            pltpu.VMEM((peers + 1, rows, LANES), jnp.float32),
            pltpu.VMEM((peers, EXTRA, LANES), jnp.float32),
            pltpu.SemaphoreType.DMA((6 + TILE_PARTS,)),
        ],
        compiler_params=params,
        name="partials",
    )(
        in_hbm(tile_dst), in_hbm(tile_slot), tile_count, in_hbm(mirror_owner), in_hbm(mirror_local),
        piece,
        *map(in_hbm, (weight, saved_agg, tile_values)),
    )
    with jax.named_scope("to_masters"):
        got = lax.all_to_all(message, "dom", 0, 0, tiled=True)
    grad_nodes, answer = pl.pallas_call(
        functools.partial(master_kernel, wide),
        out_shape=(
            jax.ShapeDtypeStruct((rows, columns), jnp.bfloat16),
            jax.ShapeDtypeStruct((peers, height, LANES), jnp.bfloat16),
        ),
        in_specs=[vmem],
        out_specs=(vmem, vmem),
        compiler_params=params,
        name="masters",
    )(got)
    with jax.named_scope("to_mirrors"):
        back = lax.all_to_all(answer, "dom", 0, 0, tiled=True)
    grad_mirrors, weight_grad = pl.pallas_call(
        functools.partial(mirror_kernel, wide),
        out_shape=(
            jax.ShapeDtypeStruct((rows, peers * LANES), jnp.bfloat16),
            jax.ShapeDtypeStruct((rows, features), jnp.float32),
        ),
        in_specs=[smem, vmem],
        out_specs=(vmem, vmem),
        compiler_params=params,
        name="mirrors",
    )(mirror_owner, back)
    return (grad_nodes, grad_mirrors, weight_grad)


def solution(mesh):
    in_specs = (
        P("feat", "dom"),
        P("feat", "dom"),
        P("feat", None),
        P("dom", None, None),
        P("dom"),
        P("dom"),
        P("dom"),
        P("dom", None),
        P("dom", None),
    )
    out_specs = (P("feat", "dom"), P("feat", "dom"), P("feat", None))
    return jax.shard_map(body, mesh=mesh, in_specs=in_specs, out_specs=out_specs, check_vma=False)
```

```python
import functools

import jax
import jax.numpy as jnp
from jax import lax
from jax.experimental import pallas as pl
from jax.experimental.pallas import tpu as pltpu
from jax.sharding import PartitionSpec as P

LANES = 128
GROUP = 96
EXTRA = 8
VMEM_BYTES = 16 * 1024 * 1024


def spread_kernel(source_hbm, copies_ref, source_ref, sem):
    move = pltpu.make_async_copy(source_hbm, source_ref, sem.at[0])
    move.start()
    move.wait()
    value = source_ref[...]
    for k in range(copies_ref.shape[0]):
        copies_ref[k] = value


def prefetch_kernel(weight_hbm, agg_hbm, tiles_hbm, weight_ref, agg_ref, tiles_ref, sems):
    pairs = ((weight_hbm, weight_ref), (agg_hbm, agg_ref), (tiles_hbm, tiles_ref))
    moves = [pltpu.make_async_copy(a, b, sems.at[k]) for k, (a, b) in enumerate(pairs)]
    for move in moves:
        move.start()
    for move in moves:
        move.wait()


def partial_kernel(
    dst_hbm, slot_hbm, count_ref, owner_hbm, local_hbm,
    piece_ref, weight_ref, agg_ref, tiles_ref,
    msg_ref,
    dst_ref, slot_ref, owner_ref, local_ref, back_ref, acc_ref, extra_ref, sems,
):
    block_count, rows, _ = back_ref.shape
    peers = msg_ref.shape[0]
    tile_total = tiles_ref.shape[0]
    wide = weight_ref.shape[1] // LANES
    pairs = (
        (dst_hbm, dst_ref), (slot_hbm, slot_ref), (owner_hbm, owner_ref), (local_hbm, local_ref),
    )
    moves = [pltpu.make_async_copy(a, b, sems.at[k]) for k, (a, b) in enumerate(pairs)]
    for move in moves:
        move.start()
    acc_ref[...] = jnp.zeros_like(acc_ref)
    piece = piece_ref[...]
    back = jnp.dot(weight_ref[...], piece, preferred_element_type=jnp.float32)
    back = back.astype(jnp.bfloat16)
    for b in range(block_count):
        back_ref[b] = back[:, b * LANES : (b + 1) * LANES]
    term = lax.dot_general(
        agg_ref[...], piece, (((1,), (1,)), ((), ())), preferred_element_type=jnp.float32
    )
    for k in range(wide):
        extra_ref[:, k, :] = term[:, k * LANES : (k + 1) * LANES]
    for k in range(wide, EXTRA):
        extra_ref[:, k, :] = jnp.zeros((peers, LANES), jnp.float32)
    for move in moves:
        move.wait()
    for s in range(peers):
        value = local_ref[0, s].astype(jnp.float32)
        extra_ref[owner_ref[0, s], pl.ds(wide, 1), :] = jnp.full((1, LANES), value, jnp.float32)
    msg_ref[:, rows:, :] = extra_ref[...].astype(jnp.bfloat16)
    count = count_ref[0]
    for start in range(0, tile_total, GROUP):
        products, places = [], []
        for t in range(start, min(start + GROUP, tile_total)):
            products.append(
                jnp.dot(back_ref[dst_ref[t]], tiles_ref[t], preferred_element_type=jnp.float32)
            )
            places.append(jnp.where(t < count, owner_ref[0, slot_ref[t]], peers))
        for place, product in zip(places, products):
            acc_ref[place] += product
    msg_ref[:, :rows, :] = acc_ref[:peers].astype(jnp.bfloat16)


def master_kernel(wide, got_ref, nodes_ref, msg_ref):
    peers, height, _ = got_ref.shape
    rows, columns = nodes_ref.shape
    block_count = columns // LANES
    tail = got_ref[:, rows:, :].astype(jnp.float32)
    numbers = [tail[p, wide : wide + 1, :] for p in range(peers)]
    sums = [jnp.zeros((rows, LANES), jnp.float32) for _ in range(block_count)]
    for p in range(peers):
        part = got_ref[p, :rows, :].astype(jnp.float32)
        for b in range(block_count):
            sums[b] = sums[b] + jnp.where(numbers[p] == float(b), part, 0.0)
    for b in range(block_count):
        nodes_ref[:, b * LANES : (b + 1) * LANES] = sums[b].astype(jnp.bfloat16)
    for p in range(peers):
        pick = sums[0]
        for b in range(1, block_count):
            pick = jnp.where(numbers[p] == float(b), sums[b], pick)
        msg_ref[p, :rows, :] = pick.astype(jnp.bfloat16)
    total = jnp.sum(tail, axis=0)
    high = total[:wide].astype(jnp.bfloat16)
    low = (total[:wide] - high.astype(jnp.float32)).astype(jnp.bfloat16)
    both = jnp.concatenate([high.astype(jnp.float32), low.astype(jnp.float32)], axis=0)
    both = both.astype(jnp.bfloat16)
    for p in range(peers):
        msg_ref[p, rows:, :] = both


def mirror_kernel(
    wide, owner_hbm, got_ref, kept_ref, mirrors_hbm, wgrad_hbm, nodes_hbm,
    owner_ref, wgrad_ref, sems,
):
    peers = got_ref.shape[0]
    rows = wgrad_ref.shape[0]
    first = pltpu.make_async_copy(owner_hbm, owner_ref, sems.at[0])
    first.start()
    moves = [pltpu.make_async_copy(kept_ref, nodes_hbm, sems.at[1])]
    moves[0].start()
    tail = got_ref[:, rows:, :].astype(jnp.float32)
    for k in range(wide):
        wgrad_ref[:, k * LANES : (k + 1) * LANES] = tail[:, k, :] + tail[:, wide + k, :]
    moves.append(pltpu.make_async_copy(wgrad_ref, wgrad_hbm, sems.at[2]))
    moves[1].start()
    first.wait()
    for s in range(peers):
        move = pltpu.make_async_copy(
            got_ref.at[owner_ref[0, s], pl.ds(0, rows), :],
            mirrors_hbm.at[:, pl.ds(s * LANES, LANES)],
            sems.at[3 + s],
        )
        move.start()
        moves.append(move)
    for move in moves:
        move.wait()


def in_hbm(array):
    return pltpu.with_memory_space_constraint(array, pltpu.HBM)


def body(
    grad_out,
    saved_agg,
    weight,
    tile_values,
    tile_dst,
    tile_slot,
    tile_count,
    mirror_owner,
    mirror_local,
):
    rows, columns = grad_out.shape
    block_count = columns // LANES
    peers = mirror_owner.shape[1]
    features = weight.shape[1]
    wide = features // LANES
    groups = features // rows
    height = rows + EXTRA
    vmem = pl.BlockSpec(memory_space=pltpu.VMEM)
    smem = pl.BlockSpec(memory_space=pltpu.SMEM)
    hbm = pl.BlockSpec(memory_space=pltpu.HBM)
    params = pltpu.CompilerParams(vmem_limit_bytes=VMEM_BYTES)

    copies = pl.pallas_call(
        spread_kernel,
        out_shape=pltpu.VMEM((groups, rows, columns), grad_out.dtype),
        in_specs=[hbm],
        out_specs=vmem,
        scratch_shapes=[pltpu.VMEM(grad_out.shape, grad_out.dtype), pltpu.SemaphoreType.DMA((1,))],
        compiler_params=params,
        name="spread",
    )(in_hbm(grad_out))
    with jax.named_scope("gather_features"):
        piece = lax.all_to_all(copies, "feat", 0, 0, tiled=True).reshape(features, columns)
    operands = (weight, saved_agg, tile_values)
    near = pl.pallas_call(
        prefetch_kernel,
        out_shape=tuple(pltpu.VMEM(x.shape, x.dtype) for x in operands),
        in_specs=[hbm] * 3,
        out_specs=(vmem,) * 3,
        scratch_shapes=[pltpu.SemaphoreType.DMA((3,))],
        compiler_params=params,
        cost_estimate=pl.CostEstimate(
            flops=0, transcendentals=0, bytes_accessed=2 * sum(x.size * 2 for x in operands)
        ),
        name="prefetch",
    )(*map(in_hbm, operands))
    message = pl.pallas_call(
        partial_kernel,
        out_shape=pltpu.VMEM((peers, height, LANES), jnp.bfloat16),
        in_specs=[hbm] * 2 + [smem] + [hbm] * 2 + [vmem] * 4,
        out_specs=vmem,
        scratch_shapes=[
            pltpu.SMEM(tile_dst.shape, jnp.int32),
            pltpu.SMEM(tile_slot.shape, jnp.int32),
            pltpu.SMEM(mirror_owner.shape, jnp.int32),
            pltpu.SMEM(mirror_local.shape, jnp.int32),
            pltpu.VMEM((block_count, rows, LANES), jnp.bfloat16),
            pltpu.VMEM((peers + 1, rows, LANES), jnp.float32),
            pltpu.VMEM((peers, EXTRA, LANES), jnp.float32),
            pltpu.SemaphoreType.DMA((4,)),
        ],
        compiler_params=params,
        name="partials",
    )(
        in_hbm(tile_dst), in_hbm(tile_slot), tile_count, in_hbm(mirror_owner), in_hbm(mirror_local),
        piece, *near,
    )
    with jax.named_scope("to_masters"):
        got = lax.all_to_all(message, "dom", 0, 0, tiled=True)
    kept, answer = pl.pallas_call(
        functools.partial(master_kernel, wide),
        out_shape=(
            pltpu.VMEM((rows, columns), jnp.bfloat16),
            pltpu.VMEM((peers, height, LANES), jnp.bfloat16),
        ),
        in_specs=[vmem],
        out_specs=(vmem, vmem),
        compiler_params=params,
        name="masters",
    )(got)
    with jax.named_scope("to_mirrors"):
        back = lax.all_to_all(answer, "dom", 0, 0, tiled=True)
    grad_mirrors, weight_grad, grad_nodes = pl.pallas_call(
        functools.partial(mirror_kernel, wide),
        out_shape=(
            pltpu.HBM((rows, peers * LANES), jnp.bfloat16),
            pltpu.HBM((rows, features), jnp.float32),
            pltpu.HBM((rows, columns), jnp.bfloat16),
        ),
        in_specs=[hbm, vmem, vmem],
        out_specs=(hbm, hbm, hbm),
        scratch_shapes=[
            pltpu.SMEM(mirror_owner.shape, jnp.int32),
            pltpu.VMEM((rows, features), jnp.float32),
            pltpu.SemaphoreType.DMA((3 + peers,)),
        ],
        compiler_params=params,
        name="mirrors",
    )(in_hbm(mirror_owner), back, kept)
    return (grad_nodes, grad_mirrors, weight_grad)


def solution(mesh):
    in_specs = (
        P("feat", "dom"),
        P("feat", "dom"),
        P("feat", None),
        P("dom", None, None),
        P("dom"),
        P("dom"),
        P("dom"),
        P("dom", None),
        P("dom", None),
    )
    out_specs = (P("feat", "dom"), P("feat", "dom"), P("feat", None))
    return jax.shard_map(body, mesh=mesh, in_specs=in_specs, out_specs=out_specs, check_vma=False)
```

```python
import functools

import jax
import jax.numpy as jnp
from jax import lax
from jax.experimental import pallas as pl
from jax.experimental.pallas import tpu as pltpu
from jax.sharding import PartitionSpec as P

LANES = 128
GROUP = 96
EXTRA = 8
VMEM_BYTES = 16 * 1024 * 1024
DOM_FIRST = 17
FEAT_FIRST = 10


def order_of(first, count):
    return [first] + [k for k in range(count) if k != first]


def place_of(index, first):
    return jnp.where(index == first, 0, index + (index < first).astype(jnp.int32))


def spread_kernel(source_hbm, copies_ref, source_ref, sem):
    move = pltpu.make_async_copy(source_hbm, source_ref, sem.at[0])
    move.start()
    move.wait()
    value = source_ref[...]
    for k in range(copies_ref.shape[0]):
        copies_ref[k] = value


def prefetch_kernel(weight_hbm, agg_hbm, tiles_hbm, weight_ref, agg_ref, tiles_ref, sems):
    pairs = ((weight_hbm, weight_ref), (agg_hbm, agg_ref), (tiles_hbm, tiles_ref))
    moves = [pltpu.make_async_copy(a, b, sems.at[k]) for k, (a, b) in enumerate(pairs)]
    for move in moves:
        move.start()
    for move in moves:
        move.wait()


def partial_kernel(
    dst_hbm, slot_hbm, count_ref, owner_hbm, local_hbm,
    piece_ref, weight_ref, agg_ref, tiles_ref,
    msg_ref,
    dst_ref, slot_ref, owner_ref, local_ref, place_ref, back_ref, acc_ref, extra_ref, sems,
):
    block_count, rows, _ = back_ref.shape
    peers = msg_ref.shape[0]
    tile_total = tiles_ref.shape[0]
    wide = weight_ref.shape[1] // LANES
    pairs = (
        (dst_hbm, dst_ref), (slot_hbm, slot_ref), (owner_hbm, owner_ref), (local_hbm, local_ref),
    )
    moves = [pltpu.make_async_copy(a, b, sems.at[k]) for k, (a, b) in enumerate(pairs)]
    for move in moves:
        move.start()
    acc_ref[...] = jnp.zeros_like(acc_ref)
    groups = piece_ref.shape[0]
    piece = jnp.concatenate(
        [piece_ref[k] for k in range(1, FEAT_FIRST + 1)]
        + [piece_ref[0]]
        + [piece_ref[k] for k in range(FEAT_FIRST + 1, groups)],
        axis=0,
    )
    back = jnp.dot(weight_ref[...], piece, preferred_element_type=jnp.float32)
    back = back.astype(jnp.bfloat16)
    for b in range(block_count):
        back_ref[b] = back[:, b * LANES : (b + 1) * LANES]
    term = lax.dot_general(
        agg_ref[...], piece, (((1,), (1,)), ((), ())), preferred_element_type=jnp.float32
    )
    for k in range(wide):
        extra_ref[:, k, :] = term[:, k * LANES : (k + 1) * LANES]
    for k in range(wide, EXTRA):
        extra_ref[:, k, :] = jnp.zeros((peers, LANES), jnp.float32)
    for move in moves:
        move.wait()
    for s in range(peers):
        value = local_ref[0, s].astype(jnp.float32)
        place = place_of(owner_ref[0, s], DOM_FIRST)
        place_ref[s] = place
        extra_ref[place, pl.ds(wide, 1), :] = jnp.full((1, LANES), value, jnp.float32)
    msg_ref[:, rows:, :] = extra_ref[...].astype(jnp.bfloat16)
    count = count_ref[0]
    for start in range(0, tile_total, GROUP):
        products, places = [], []
        for t in range(start, min(start + GROUP, tile_total)):
            products.append(
                jnp.dot(back_ref[dst_ref[t]], tiles_ref[t], preferred_element_type=jnp.float32)
            )
            places.append(jnp.where(t < count, place_ref[slot_ref[t]], peers))
        for place, product in zip(places, products):
            acc_ref[place] += product
    msg_ref[:, :rows, :] = acc_ref[:peers].astype(jnp.bfloat16)


def master_kernel(wide, got_ref, nodes_ref, msg_ref):
    peers, height, _ = got_ref.shape
    rows, columns = nodes_ref.shape
    block_count = columns // LANES
    tail = got_ref[:, rows:, :].astype(jnp.float32)
    numbers = [tail[p, wide : wide + 1, :] for p in range(peers)]
    sums = [jnp.zeros((rows, LANES), jnp.float32) for _ in range(block_count)]
    for p in range(peers):
        part = got_ref[p, :rows, :].astype(jnp.float32)
        for b in range(block_count):
            sums[b] = sums[b] + jnp.where(numbers[p] == float(b), part, 0.0)
    for b in range(block_count):
        nodes_ref[:, b * LANES : (b + 1) * LANES] = sums[b].astype(jnp.bfloat16)
    for p in range(peers):
        pick = sums[0]
        for b in range(1, block_count):
            pick = jnp.where(numbers[p] == float(b), sums[b], pick)
        msg_ref[p, :rows, :] = pick.astype(jnp.bfloat16)
    total = jnp.sum(tail, axis=0)
    high = total[:wide].astype(jnp.bfloat16)
    low = (total[:wide] - high.astype(jnp.float32)).astype(jnp.bfloat16)
    both = jnp.concatenate([high.astype(jnp.float32), low.astype(jnp.float32)], axis=0)
    both = both.astype(jnp.bfloat16)
    for p in range(peers):
        msg_ref[p, rows:, :] = both


def mirror_kernel(
    wide, owner_hbm, got_ref, kept_ref, mirrors_hbm, wgrad_hbm, nodes_hbm,
    owner_ref, wgrad_ref, sems,
):
    peers = got_ref.shape[0]
    rows = wgrad_ref.shape[0]
    first = pltpu.make_async_copy(owner_hbm, owner_ref, sems.at[0])
    first.start()
    moves = [pltpu.make_async_copy(kept_ref, nodes_hbm, sems.at[1])]
    moves[0].start()
    tail = got_ref[:, rows:, :].astype(jnp.float32)
    for k in range(wide):
        wgrad_ref[:, k * LANES : (k + 1) * LANES] = tail[:, k, :] + tail[:, wide + k, :]
    moves.append(pltpu.make_async_copy(wgrad_ref, wgrad_hbm, sems.at[2]))
    moves[1].start()
    first.wait()
    for s in range(peers):
        move = pltpu.make_async_copy(
            got_ref.at[place_of(owner_ref[0, s], DOM_FIRST), pl.ds(0, rows), :],
            mirrors_hbm.at[:, pl.ds(s * LANES, LANES)],
            sems.at[3 + s],
        )
        move.start()
        moves.append(move)
    for move in moves:
        move.wait()


def in_hbm(array):
    return pltpu.with_memory_space_constraint(array, pltpu.HBM)


def body(
    grad_out,
    saved_agg,
    weight,
    tile_values,
    tile_dst,
    tile_slot,
    tile_count,
    mirror_owner,
    mirror_local,
):
    rows, columns = grad_out.shape
    block_count = columns // LANES
    peers = mirror_owner.shape[1]
    features = weight.shape[1]
    wide = features // LANES
    groups = features // rows
    height = rows + EXTRA
    dom_groups = [order_of(DOM_FIRST, peers)]
    vmem = pl.BlockSpec(memory_space=pltpu.VMEM)
    smem = pl.BlockSpec(memory_space=pltpu.SMEM)
    hbm = pl.BlockSpec(memory_space=pltpu.HBM)
    params = pltpu.CompilerParams(vmem_limit_bytes=VMEM_BYTES)

    copies = pl.pallas_call(
        spread_kernel,
        out_shape=pltpu.VMEM((groups, rows, columns), grad_out.dtype),
        in_specs=[hbm],
        out_specs=vmem,
        scratch_shapes=[pltpu.VMEM(grad_out.shape, grad_out.dtype), pltpu.SemaphoreType.DMA((1,))],
        compiler_params=params,
        name="spread",
    )(in_hbm(grad_out))
    with jax.named_scope("gather_features"):
        piece = lax.all_to_all(
            copies, "feat", 0, 0, tiled=True, axis_index_groups=[order_of(FEAT_FIRST, groups)]
        )
    operands = (weight, saved_agg, tile_values)
    near = pl.pallas_call(
        prefetch_kernel,
        out_shape=tuple(pltpu.VMEM(x.shape, x.dtype) for x in operands),
        in_specs=[hbm] * 3,
        out_specs=(vmem,) * 3,
        scratch_shapes=[pltpu.SemaphoreType.DMA((3,))],
        compiler_params=params,
        cost_estimate=pl.CostEstimate(
            flops=0, transcendentals=0, bytes_accessed=2 * sum(x.size * 2 for x in operands)
        ),
        name="prefetch",
    )(*map(in_hbm, operands))
    message = pl.pallas_call(
        partial_kernel,
        out_shape=pltpu.VMEM((peers, height, LANES), jnp.bfloat16),
        in_specs=[hbm] * 2 + [smem] + [hbm] * 2 + [vmem] * 4,
        out_specs=vmem,
        scratch_shapes=[
            pltpu.SMEM(tile_dst.shape, jnp.int32),
            pltpu.SMEM(tile_slot.shape, jnp.int32),
            pltpu.SMEM(mirror_owner.shape, jnp.int32),
            pltpu.SMEM(mirror_local.shape, jnp.int32),
            pltpu.SMEM((peers,), jnp.int32),
            pltpu.VMEM((block_count, rows, LANES), jnp.bfloat16),
            pltpu.VMEM((peers + 1, rows, LANES), jnp.float32),
            pltpu.VMEM((peers, EXTRA, LANES), jnp.float32),
            pltpu.SemaphoreType.DMA((4,)),
        ],
        compiler_params=params,
        name="partials",
    )(
        in_hbm(tile_dst), in_hbm(tile_slot), tile_count, in_hbm(mirror_owner), in_hbm(mirror_local),
        piece, *near,
    )
    with jax.named_scope("to_masters"):
        got = lax.all_to_all(message, "dom", 0, 0, tiled=True, axis_index_groups=dom_groups)
    kept, answer = pl.pallas_call(
        functools.partial(master_kernel, wide),
        out_shape=(
            pltpu.VMEM((rows, columns), jnp.bfloat16),
            pltpu.VMEM((peers, height, LANES), jnp.bfloat16),
        ),
        in_specs=[vmem],
        out_specs=(vmem, vmem),
        compiler_params=params,
        name="masters",
    )(got)
    with jax.named_scope("to_mirrors"):
        back = lax.all_to_all(answer, "dom", 0, 0, tiled=True, axis_index_groups=dom_groups)
    grad_mirrors, weight_grad, grad_nodes = pl.pallas_call(
        functools.partial(mirror_kernel, wide),
        out_shape=(
            pltpu.HBM((rows, peers * LANES), jnp.bfloat16),
            pltpu.HBM((rows, features), jnp.float32),
            pltpu.HBM((rows, columns), jnp.bfloat16),
        ),
        in_specs=[hbm, vmem, vmem],
        out_specs=(hbm, hbm, hbm),
        scratch_shapes=[
            pltpu.SMEM(mirror_owner.shape, jnp.int32),
            pltpu.VMEM((rows, features), jnp.float32),
            pltpu.SemaphoreType.DMA((3 + peers,)),
        ],
        compiler_params=params,
        name="mirrors",
    )(in_hbm(mirror_owner), back, kept)
    return (grad_nodes, grad_mirrors, weight_grad)


def solution(mesh):
    in_specs = (
        P("feat", "dom"),
        P("feat", "dom"),
        P("feat", None),
        P("dom", None, None),
        P("dom"),
        P("dom"),
        P("dom"),
        P("dom", None),
        P("dom", None),
    )
    out_specs = (P("feat", "dom"), P("feat", "dom"), P("feat", None))
    return jax.shard_map(body, mesh=mesh, in_specs=in_specs, out_specs=out_specs, check_vma=False)
```

```python
import functools

import jax
import jax.numpy as jnp
from jax import lax
from jax.experimental import pallas as pl
from jax.experimental.pallas import tpu as pltpu
from jax.sharding import PartitionSpec as P

LANES = 128
GROUP = 16
EARLY = 80
EXTRA = 6
VMEM_BYTES = 16 * 1024 * 1024
DOM_FIRST = 17
FEAT_FIRST = 10


def order_of(first, count):
    return [first] + [k for k in range(count) if k != first]


def place_of(index, first):
    return jnp.where(index == first, 0, index + (index < first).astype(jnp.int32))


def spread_kernel(source_hbm, copies_ref, source_ref, sem):
    move = pltpu.make_async_copy(source_hbm, source_ref, sem.at[0])
    move.start()
    move.wait()
    value = source_ref[...]
    for k in range(copies_ref.shape[0]):
        copies_ref[k] = value


def prefetch_kernel(
    dst_hbm, slot_hbm, count_ref, owner_hbm, local_hbm, weight_hbm, agg_hbm, tiles_hbm,
    dst_ref, place_ref, peer_ref, number_ref, weight_ref, agg_ref, tiles_ref,
    slot_ref, owner_ref, local_ref, sems,
):
    pairs = (
        (owner_hbm, owner_ref), (local_hbm, local_ref), (slot_hbm, slot_ref), (dst_hbm, dst_ref),
        (weight_hbm, weight_ref), (agg_hbm, agg_ref), (tiles_hbm.at[pl.ds(0, EARLY)], tiles_ref),
    )
    moves = [pltpu.make_async_copy(a, b, sems.at[k]) for k, (a, b) in enumerate(pairs)]
    for move in moves:
        move.start()
    peers = peer_ref.shape[0]
    tile_total = place_ref.shape[0]
    moves[0].wait()
    moves[1].wait()

    def slot_step(s, carry):
        place = place_of(owner_ref[0, s], DOM_FIRST)
        peer_ref[s] = place
        number_ref[place] = local_ref[0, s]
        return carry

    lax.fori_loop(0, peers, slot_step, 0)
    moves[2].wait()
    count = count_ref[0]

    def tile_step(t, carry):
        place_ref[t] = jnp.where(t < count, peer_ref[slot_ref[t]], peers)
        return carry

    lax.fori_loop(0, tile_total, tile_step, 0)
    for move in moves[3:]:
        move.wait()


def partial_kernel(
    dst_ref, place_ref, number_ref, piece_ref, weight_ref, agg_ref, early_ref, tiles_hbm,
    msg_ref,
    back_ref, acc_ref, extra_ref, late_ref, sems,
):
    block_count, rows, _ = back_ref.shape
    peers = msg_ref.shape[0]
    msg_ref = msg_ref.reshape(peers, msg_ref.shape[1] * msg_ref.shape[2], LANES)
    tile_total = tiles_hbm.shape[0]
    wide = weight_ref.shape[1] // LANES
    late = pltpu.make_async_copy(
        tiles_hbm.at[pl.ds(EARLY, tile_total - EARLY)], late_ref, sems.at[0]
    )
    late.start()
    acc_ref[...] = jnp.zeros_like(acc_ref)
    groups = piece_ref.shape[0]
    piece = jnp.concatenate(
        [piece_ref[k] for k in range(1, FEAT_FIRST + 1)]
        + [piece_ref[0]]
        + [piece_ref[k] for k in range(FEAT_FIRST + 1, groups)],
        axis=0,
    )
    back = jnp.dot(weight_ref[...], piece, preferred_element_type=jnp.float32)
    back = back.astype(jnp.bfloat16)
    for b in range(block_count):
        back_ref[b] = back[:, b * LANES : (b + 1) * LANES]
    term = lax.dot_general(
        agg_ref[...], piece, (((1,), (1,)), ((), ())), preferred_element_type=jnp.float32
    )
    for k in range(wide):
        extra_ref[:, k, :] = term[:, k * LANES : (k + 1) * LANES]
    extra_ref[:, wide:, :] = jnp.zeros_like(extra_ref[:, wide:, :])
    for k in range(peers):
        value = number_ref[k].astype(jnp.float32)
        extra_ref[k, pl.ds(wide, 1), :] = jnp.full((1, LANES), value, jnp.float32)
    msg_ref[:, rows:, :] = extra_ref[:, :EXTRA, :].astype(jnp.bfloat16)
    for start in range(0, tile_total, GROUP):
        if start == EARLY:
            late.wait()
        products, places = [], []
        for t in range(start, min(start + GROUP, tile_total)):
            tile = early_ref[t] if t < EARLY else late_ref[t - EARLY]
            products.append(
                jnp.dot(back_ref[dst_ref[t]], tile, preferred_element_type=jnp.float32)
            )
            places.append(place_ref[t])
        for place, product in zip(places, products):
            acc_ref[place] += product
    msg_ref[:, :rows, :] = acc_ref[:peers].astype(jnp.bfloat16)


def master_kernel(wide, got_ref, nodes_ref, msg_ref):
    peers = got_ref.shape[0]
    got_ref = got_ref.reshape(peers, got_ref.shape[1] * got_ref.shape[2], LANES)
    rows, columns = nodes_ref.shape
    block_count = columns // LANES
    msg_ref = msg_ref.reshape(peers, rows + wide, LANES)
    tail = got_ref[:, rows:, :].astype(jnp.float32)
    numbers = [tail[p, wide : wide + 1, :] for p in range(peers)]
    sums = [jnp.zeros((rows, LANES), jnp.float32) for _ in range(block_count)]
    for p in range(peers):
        part = got_ref[p, :rows, :].astype(jnp.float32)
        for b in range(block_count):
            sums[b] = sums[b] + jnp.where(numbers[p] == float(b), part, 0.0)
    for b in range(block_count):
        nodes_ref[:, b * LANES : (b + 1) * LANES] = sums[b].astype(jnp.bfloat16)
    for p in range(peers):
        pick = sums[0]
        for b in range(1, block_count):
            pick = jnp.where(numbers[p] == float(b), sums[b], pick)
        msg_ref[p, :rows, :] = pick.astype(jnp.bfloat16)
    total = jnp.sum(tail, axis=0)[:wide].astype(jnp.bfloat16)
    for p in range(peers):
        msg_ref[p, rows:, :] = total


def mirror_kernel(
    wide, peer_ref, got_ref, kept_ref, mirrors_hbm, wgrad_hbm, nodes_hbm,
    wgrad_ref, mirrors_ref, sems,
):
    peers = got_ref.shape[0]
    rows = wgrad_ref.shape[0]
    got_ref = got_ref.reshape(peers, rows + wide, LANES)
    moves = [pltpu.make_async_copy(kept_ref, nodes_hbm, sems.at[1])]
    moves[0].start()
    tail = got_ref[:, rows:, :].astype(jnp.float32)
    for k in range(wide):
        wgrad_ref[:, k * LANES : (k + 1) * LANES] = tail[:, k, :]
    moves.append(pltpu.make_async_copy(wgrad_ref, wgrad_hbm, sems.at[2]))
    moves[1].start()
    part = peers // 2
    for c in range(2):
        for s in range(c * part, (c + 1) * part):
            mirrors_ref[:, s * LANES : (s + 1) * LANES] = got_ref[peer_ref[s], :rows, :]
        span = pl.ds(c * part * LANES, part * LANES)
        move = pltpu.make_async_copy(mirrors_ref.at[:, span], mirrors_hbm.at[:, span], sems.at[3 + c])
        move.start()
        moves.append(move)
    for move in moves:
        move.wait()


def in_hbm(array):
    return pltpu.with_memory_space_constraint(array, pltpu.HBM)


def in_vmem(array):
    return pltpu.with_memory_space_constraint(array, pltpu.VMEM)


def body(
    grad_out,
    saved_agg,
    weight,
    tile_values,
    tile_dst,
    tile_slot,
    tile_count,
    mirror_owner,
    mirror_local,
):
    rows, columns = grad_out.shape
    block_count = columns // LANES
    peers = mirror_owner.shape[1]
    features = weight.shape[1]
    wide = features // LANES
    groups = features // rows
    height = rows + EXTRA
    dom_groups = [order_of(DOM_FIRST, peers)]
    vmem = pl.BlockSpec(memory_space=pltpu.VMEM)
    smem = pl.BlockSpec(memory_space=pltpu.SMEM)
    hbm = pl.BlockSpec(memory_space=pltpu.HBM)
    params = pltpu.CompilerParams(vmem_limit_bytes=VMEM_BYTES)

    copies = pl.pallas_call(
        spread_kernel,
        out_shape=pltpu.VMEM((groups, rows, columns), grad_out.dtype),
        in_specs=[hbm],
        out_specs=vmem,
        scratch_shapes=[pltpu.VMEM(grad_out.shape, grad_out.dtype), pltpu.SemaphoreType.DMA((1,))],
        compiler_params=params,
        name="spread",
    )(in_hbm(grad_out))
    with jax.named_scope("gather_features"):
        piece = lax.all_to_all(
            copies, "feat", 0, 0, tiled=True, axis_index_groups=[order_of(FEAT_FIRST, groups)]
        )
    operands = (weight, saved_agg, tile_values)
    dst, place, peer, number, *near = pl.pallas_call(
        prefetch_kernel,
        out_shape=(
            pltpu.SMEM(tile_dst.shape, jnp.int32),
            pltpu.SMEM(tile_slot.shape, jnp.int32),
            pltpu.SMEM((peers,), jnp.int32),
            pltpu.SMEM((peers,), jnp.int32),
            *(pltpu.VMEM(x.shape, x.dtype) for x in operands[:2]),
            pltpu.VMEM((EARLY, LANES, LANES), tile_values.dtype),
        ),
        in_specs=[hbm] * 2 + [smem] + [hbm] * 5,
        out_specs=(smem,) * 4 + (vmem,) * 3,
        scratch_shapes=[
            pltpu.SMEM(tile_slot.shape, jnp.int32),
            pltpu.SMEM(mirror_owner.shape, jnp.int32),
            pltpu.SMEM(mirror_local.shape, jnp.int32),
            pltpu.SemaphoreType.DMA((7,)),
        ],
        compiler_params=params,
        cost_estimate=pl.CostEstimate(
            flops=0, transcendentals=0, bytes_accessed=2 * sum(x.size * 2 for x in operands)
        ),
        name="prefetch",
    )(
        in_hbm(tile_dst), in_hbm(tile_slot), tile_count, in_hbm(mirror_owner), in_hbm(mirror_local),
        *map(in_hbm, operands),
    )
    message = pl.pallas_call(
        partial_kernel,
        out_shape=pltpu.VMEM((peers, height // 2, 2, LANES), jnp.bfloat16),
        in_specs=[smem] * 3 + [vmem] * 4 + [hbm],
        out_specs=vmem,
        scratch_shapes=[
            pltpu.VMEM((block_count, rows, LANES), jnp.bfloat16),
            pltpu.VMEM((peers + 1, rows, LANES), jnp.float32),
            pltpu.VMEM((peers, 8, LANES), jnp.float32),
            pltpu.VMEM((tile_values.shape[0] - EARLY, LANES, LANES), tile_values.dtype),
            pltpu.SemaphoreType.DMA((1,)),
        ],
        compiler_params=params,
        name="partials",
    )(dst, place, number, piece, *map(in_vmem, near), in_hbm(tile_values))
    with jax.named_scope("to_masters"):
        got = lax.all_to_all(message, "dom", 0, 0, tiled=True, axis_index_groups=dom_groups)
    kept, answer = pl.pallas_call(
        functools.partial(master_kernel, wide),
        out_shape=(
            pltpu.VMEM((rows, columns), jnp.bfloat16),
            pltpu.VMEM((peers, (rows + wide) // wide, wide, LANES), jnp.bfloat16),
        ),
        in_specs=[vmem],
        out_specs=(vmem, vmem),
        compiler_params=params,
        name="masters",
    )(got)
    with jax.named_scope("to_mirrors"):
        back = lax.all_to_all(answer, "dom", 0, 0, tiled=True, axis_index_groups=dom_groups)
    grad_mirrors, weight_grad, grad_nodes = pl.pallas_call(
        functools.partial(mirror_kernel, wide),
        out_shape=(
            pltpu.HBM((rows, peers * LANES), jnp.bfloat16),
            pltpu.HBM((rows, features), jnp.float32),
            pltpu.HBM((rows, columns), jnp.bfloat16),
        ),
        in_specs=[smem, vmem, vmem],
        out_specs=(hbm, hbm, hbm),
        scratch_shapes=[
            pltpu.VMEM((rows, features), jnp.float32),
            pltpu.VMEM((rows, peers * LANES), jnp.bfloat16),
            pltpu.SemaphoreType.DMA((3 + 2,)),
        ],
        compiler_params=params,
        name="mirrors",
    )(peer, back, kept)
    return (grad_nodes, grad_mirrors, weight_grad)


def solution(mesh):
    in_specs = (
        P("feat", "dom"),
        P("feat", "dom"),
        P("feat", None),
        P("dom", None, None),
        P("dom"),
        P("dom"),
        P("dom"),
        P("dom", None),
        P("dom", None),
    )
    out_specs = (P("feat", "dom"), P("feat", "dom"), P("feat", None))
    return jax.shard_map(body, mesh=mesh, in_specs=in_specs, out_specs=out_specs, check_vma=False)
```

```python
import functools

import jax
import jax.numpy as jnp
from jax import lax
from jax.experimental import pallas as pl
from jax.experimental.pallas import tpu as pltpu
from jax.sharding import PartitionSpec as P

LANES = 128
GROUP = 40
EARLY = 80
EXTRA = 6
VMEM_BYTES = 16 * 1024 * 1024
DOM_FIRST = 17
FEAT_FIRST = 10


def order_of(first, count):
    return [first] + [k for k in range(count) if k != first]


def place_of(index, first):
    return jnp.where(index == first, 0, index + (index < first).astype(jnp.int32))


def spread_kernel(source_hbm, copies_ref, source_ref, sem):
    move = pltpu.make_async_copy(source_hbm, source_ref, sem.at[0])
    move.start()
    move.wait()
    value = source_ref[...]
    for k in range(copies_ref.shape[0]):
        copies_ref[k] = value


def prefetch_kernel(
    dst_hbm, slot_hbm, count_ref, owner_hbm, local_hbm, weight_hbm, agg_hbm, tiles_hbm,
    dst_ref, place_ref, peer_ref, number_ref, weight_ref, agg_ref, tiles_ref,
    slot_ref, owner_ref, local_ref, sems,
):
    pairs = (
        (owner_hbm, owner_ref), (local_hbm, local_ref), (slot_hbm, slot_ref), (dst_hbm, dst_ref),
        (weight_hbm, weight_ref), (agg_hbm, agg_ref), (tiles_hbm.at[pl.ds(0, EARLY)], tiles_ref),
    )
    moves = [pltpu.make_async_copy(a, b, sems.at[k]) for k, (a, b) in enumerate(pairs)]
    for move in moves:
        move.start()
    peers = peer_ref.shape[0]
    tile_total = place_ref.shape[0]
    moves[0].wait()
    moves[1].wait()

    def slot_step(s, carry):
        place = place_of(owner_ref[0, s], DOM_FIRST)
        peer_ref[s] = place
        number_ref[place] = local_ref[0, s]
        return carry

    lax.fori_loop(0, peers, slot_step, 0)
    moves[2].wait()
    count = count_ref[0]

    def tile_step(t, carry):
        place_ref[t] = jnp.where(t < count, peer_ref[slot_ref[t]], peers)
        return carry

    lax.fori_loop(0, tile_total, tile_step, 0)
    for move in moves[3:]:
        move.wait()


def partial_kernel(
    dst_ref, place_ref, number_ref, piece_ref, weight_ref, agg_ref, early_ref, tiles_hbm,
    msg_ref,
    back_ref, acc_ref, extra_ref, late_ref, sems,
):
    block_count, rows, _ = back_ref.shape
    peers = msg_ref.shape[0]
    msg_ref = msg_ref.reshape(peers, msg_ref.shape[1] * msg_ref.shape[2], LANES)
    tile_total = tiles_hbm.shape[0]
    wide = weight_ref.shape[1] // LANES
    late = pltpu.make_async_copy(
        tiles_hbm.at[pl.ds(EARLY, tile_total - EARLY)], late_ref, sems.at[0]
    )
    late.start()
    acc_ref[...] = jnp.zeros_like(acc_ref)
    groups = piece_ref.shape[0]
    piece = jnp.concatenate(
        [piece_ref[k] for k in range(1, FEAT_FIRST + 1)]
        + [piece_ref[0]]
        + [piece_ref[k] for k in range(FEAT_FIRST + 1, groups)],
        axis=0,
    )
    back = jnp.dot(weight_ref[...], piece, preferred_element_type=jnp.float32)
    back = back.astype(jnp.bfloat16)
    for b in range(block_count):
        back_ref[b] = back[:, b * LANES : (b + 1) * LANES]
    term = lax.dot_general(
        agg_ref[...], piece, (((1,), (1,)), ((), ())), preferred_element_type=jnp.float32
    )
    for k in range(wide):
        extra_ref[:, k, :] = term[:, k * LANES : (k + 1) * LANES]
    extra_ref[:, wide:, :] = jnp.zeros_like(extra_ref[:, wide:, :])
    for k in range(peers):
        value = number_ref[k].astype(jnp.float32)
        extra_ref[k, pl.ds(wide, 1), :] = jnp.full((1, LANES), value, jnp.float32)
    msg_ref[:, rows:, :] = extra_ref[:, :EXTRA, :].astype(jnp.bfloat16)
    def add_tiles(start, count, tiles_ref, skip):
        products, places = [], []
        for t in range(count):
            products.append(
                jnp.dot(
                    back_ref[dst_ref[start + t]], tiles_ref[start + t - skip],
                    preferred_element_type=jnp.float32,
                )
            )
            places.append(place_ref[start + t])
        for place, product in zip(places, products):
            acc_ref[place] += product

    def step(i, carry):
        add_tiles(i * GROUP, GROUP, early_ref, 0)
        return carry

    lax.fori_loop(0, EARLY // GROUP, step, 0)
    late.wait()
    add_tiles(EARLY, tile_total - EARLY, late_ref, EARLY)
    msg_ref[:, :rows, :] = acc_ref[:peers].astype(jnp.bfloat16)


def master_kernel(wide, got_ref, nodes_ref, msg_ref):
    peers = got_ref.shape[0]
    got_ref = got_ref.reshape(peers, got_ref.shape[1] * got_ref.shape[2], LANES)
    rows, columns = nodes_ref.shape
    block_count = columns // LANES
    msg_ref = msg_ref.reshape(peers, rows + wide, LANES)
    tail = got_ref[:, rows:, :].astype(jnp.float32)
    numbers = [tail[p, wide : wide + 1, :] for p in range(peers)]
    sums = [jnp.zeros((rows, LANES), jnp.float32) for _ in range(block_count)]
    for p in range(peers):
        part = got_ref[p, :rows, :].astype(jnp.float32)
        for b in range(block_count):
            sums[b] = sums[b] + jnp.where(numbers[p] == float(b), part, 0.0)
    for b in range(block_count):
        nodes_ref[:, b * LANES : (b + 1) * LANES] = sums[b].astype(jnp.bfloat16)
    for p in range(peers):
        pick = sums[0]
        for b in range(1, block_count):
            pick = jnp.where(numbers[p] == float(b), sums[b], pick)
        msg_ref[p, :rows, :] = pick.astype(jnp.bfloat16)
    total = jnp.sum(tail, axis=0)[:wide].astype(jnp.bfloat16)
    for p in range(peers):
        msg_ref[p, rows:, :] = total


def mirror_kernel(
    wide, peer_ref, got_ref, kept_ref, mirrors_hbm, wgrad_hbm, nodes_hbm,
    wgrad_ref, mirrors_ref, sems,
):
    peers = got_ref.shape[0]
    rows = wgrad_ref.shape[0]
    got_ref = got_ref.reshape(peers, rows + wide, LANES)
    moves = [pltpu.make_async_copy(kept_ref, nodes_hbm, sems.at[1])]
    moves[0].start()
    tail = got_ref[:, rows:, :].astype(jnp.float32)
    for k in range(wide):
        wgrad_ref[:, k * LANES : (k + 1) * LANES] = tail[:, k, :]
    moves.append(pltpu.make_async_copy(wgrad_ref, wgrad_hbm, sems.at[2]))
    moves[1].start()
    part = peers // 2
    for c in range(2):
        for s in range(c * part, (c + 1) * part):
            mirrors_ref[:, s * LANES : (s + 1) * LANES] = got_ref[peer_ref[s], :rows, :]
        span = pl.ds(c * part * LANES, part * LANES)
        move = pltpu.make_async_copy(mirrors_ref.at[:, span], mirrors_hbm.at[:, span], sems.at[3 + c])
        move.start()
        moves.append(move)
    for move in moves:
        move.wait()


def in_hbm(array):
    return pltpu.with_memory_space_constraint(array, pltpu.HBM)


def in_vmem(array):
    return pltpu.with_memory_space_constraint(array, pltpu.VMEM)


def body(
    grad_out,
    saved_agg,
    weight,
    tile_values,
    tile_dst,
    tile_slot,
    tile_count,
    mirror_owner,
    mirror_local,
):
    rows, columns = grad_out.shape
    block_count = columns // LANES
    peers = mirror_owner.shape[1]
    features = weight.shape[1]
    wide = features // LANES
    groups = features // rows
    height = rows + EXTRA
    dom_groups = [order_of(DOM_FIRST, peers)]
    vmem = pl.BlockSpec(memory_space=pltpu.VMEM)
    smem = pl.BlockSpec(memory_space=pltpu.SMEM)
    hbm = pl.BlockSpec(memory_space=pltpu.HBM)
    params = pltpu.CompilerParams(vmem_limit_bytes=VMEM_BYTES)

    copies = pl.pallas_call(
        spread_kernel,
        out_shape=pltpu.VMEM((groups, rows, columns), grad_out.dtype),
        in_specs=[hbm],
        out_specs=vmem,
        scratch_shapes=[pltpu.VMEM(grad_out.shape, grad_out.dtype), pltpu.SemaphoreType.DMA((1,))],
        compiler_params=params,
        name="spread",
    )(in_hbm(grad_out))
    with jax.named_scope("gather_features"):
        piece = lax.all_to_all(
            copies, "feat", 0, 0, tiled=True, axis_index_groups=[order_of(FEAT_FIRST, groups)]
        )
    operands = (weight, saved_agg, tile_values)
    dst, place, peer, number, *near = pl.pallas_call(
        prefetch_kernel,
        out_shape=(
            pltpu.SMEM(tile_dst.shape, jnp.int32),
            pltpu.SMEM(tile_slot.shape, jnp.int32),
            pltpu.SMEM((peers,), jnp.int32),
            pltpu.SMEM((peers,), jnp.int32),
            *(pltpu.VMEM(x.shape, x.dtype) for x in operands[:2]),
            pltpu.VMEM((EARLY, LANES, LANES), tile_values.dtype),
        ),
        in_specs=[hbm] * 2 + [smem] + [hbm] * 5,
        out_specs=(smem,) * 4 + (vmem,) * 3,
        scratch_shapes=[
            pltpu.SMEM(tile_slot.shape, jnp.int32),
            pltpu.SMEM(mirror_owner.shape, jnp.int32),
            pltpu.SMEM(mirror_local.shape, jnp.int32),
            pltpu.SemaphoreType.DMA((7,)),
        ],
        compiler_params=params,
        cost_estimate=pl.CostEstimate(
            flops=0, transcendentals=0, bytes_accessed=2 * sum(x.size * 2 for x in operands)
        ),
        name="prefetch",
    )(
        in_hbm(tile_dst), in_hbm(tile_slot), tile_count, in_hbm(mirror_owner), in_hbm(mirror_local),
        *map(in_hbm, operands),
    )
    message = pl.pallas_call(
        partial_kernel,
        out_shape=pltpu.VMEM((peers, height // 2, 2, LANES), jnp.bfloat16),
        in_specs=[smem] * 3 + [vmem] * 4 + [hbm],
        out_specs=vmem,
        scratch_shapes=[
            pltpu.VMEM((block_count, rows, LANES), jnp.bfloat16),
            pltpu.VMEM((peers + 1, rows, LANES), jnp.float32),
            pltpu.VMEM((peers, 8, LANES), jnp.float32),
            pltpu.VMEM((tile_values.shape[0] - EARLY, LANES, LANES), tile_values.dtype),
            pltpu.SemaphoreType.DMA((1,)),
        ],
        compiler_params=params,
        name="partials",
    )(dst, place, number, piece, *map(in_vmem, near), in_hbm(tile_values))
    with jax.named_scope("to_masters"):
        got = lax.all_to_all(message, "dom", 0, 0, tiled=True, axis_index_groups=dom_groups)
    kept, answer = pl.pallas_call(
        functools.partial(master_kernel, wide),
        out_shape=(
            pltpu.VMEM((rows, columns), jnp.bfloat16),
            pltpu.VMEM((peers, (rows + wide) // wide, wide, LANES), jnp.bfloat16),
        ),
        in_specs=[vmem],
        out_specs=(vmem, vmem),
        compiler_params=params,
        name="masters",
    )(got)
    with jax.named_scope("to_mirrors"):
        back = lax.all_to_all(answer, "dom", 0, 0, tiled=True, axis_index_groups=dom_groups)
    grad_mirrors, weight_grad, grad_nodes = pl.pallas_call(
        functools.partial(mirror_kernel, wide),
        out_shape=(
            pltpu.HBM((rows, peers * LANES), jnp.bfloat16),
            pltpu.HBM((rows, features), jnp.float32),
            pltpu.HBM((rows, columns), jnp.bfloat16),
        ),
        in_specs=[smem, vmem, vmem],
        out_specs=(hbm, hbm, hbm),
        scratch_shapes=[
            pltpu.VMEM((rows, features), jnp.float32),
            pltpu.VMEM((rows, peers * LANES), jnp.bfloat16),
            pltpu.SemaphoreType.DMA((3 + 2,)),
        ],
        compiler_params=params,
        name="mirrors",
    )(peer, back, kept)
    return (grad_nodes, grad_mirrors, weight_grad)


def solution(mesh):
    in_specs = (
        P("feat", "dom"),
        P("feat", "dom"),
        P("feat", None),
        P("dom", None, None),
        P("dom"),
        P("dom"),
        P("dom"),
        P("dom", None),
        P("dom", None),
    )
    out_specs = (P("feat", "dom"), P("feat", "dom"), P("feat", None))
    return jax.shard_map(body, mesh=mesh, in_specs=in_specs, out_specs=out_specs, check_vma=False)
```

```python
import functools

import jax
import jax.numpy as jnp
from jax import lax
from jax.experimental import pallas as pl
from jax.experimental.pallas import tpu as pltpu
from jax.sharding import PartitionSpec as P

LANES = 128
GROUP = 48
EXTRA = 6
VMEM_BYTES = 16 * 1024 * 1024
DOM_FIRST = 17
FEAT_FIRST = 10


def order_of(first, count):
    return [first] + [k for k in range(count) if k != first]


def place_of(index, first):
    return jnp.where(index == first, 0, index + (index < first).astype(jnp.int32))


def stage_kernel(
    grad_hbm, dst_hbm, slot_hbm, count_ref, owner_hbm, local_hbm, weight_hbm, agg_hbm, tiles_hbm,
    copies_ref, dst_ref, place_ref, peer_ref, number_ref, weight_ref, agg_ref, tiles_ref,
    grad_ref, slot_ref, owner_ref, local_ref, sems,
):
    pairs = (
        (grad_hbm, grad_ref), (owner_hbm, owner_ref), (local_hbm, local_ref),
        (slot_hbm, slot_ref), (dst_hbm, dst_ref),
        (weight_hbm, weight_ref), (agg_hbm, agg_ref), (tiles_hbm, tiles_ref),
    )
    moves = [pltpu.make_async_copy(a, b, sems.at[k]) for k, (a, b) in enumerate(pairs)]
    for move in moves:
        move.start()
    peers = peer_ref.shape[0]
    tile_total = place_ref.shape[0]
    moves[0].wait()
    value = grad_ref[...]
    for k in range(copies_ref.shape[0]):
        copies_ref[k] = value
    moves[1].wait()
    moves[2].wait()

    def slot_step(s, carry):
        place = place_of(owner_ref[0, s], DOM_FIRST)
        peer_ref[s] = place
        number_ref[place] = local_ref[0, s]
        return carry

    lax.fori_loop(0, peers, slot_step, 0, unroll=8)
    moves[3].wait()
    count = count_ref[0]

    def tile_step(t, carry):
        place_ref[t] = jnp.where(t < count, peer_ref[slot_ref[t]], peers)
        return carry

    lax.fori_loop(0, tile_total, tile_step, 0, unroll=8)
    for move in moves[4:]:
        move.wait()


def partial_kernel(
    dst_ref, place_ref, number_ref, piece_ref, weight_ref, agg_ref, tiles_ref,
    msg_ref,
    back_ref, acc_ref, extra_ref,
):
    block_count, rows, _ = back_ref.shape
    peers = msg_ref.shape[0]
    msg_ref = msg_ref.reshape(peers, msg_ref.shape[1] * msg_ref.shape[2], LANES)
    tile_total = tiles_ref.shape[0]
    wide = weight_ref.shape[1] // LANES
    acc_ref[...] = jnp.zeros_like(acc_ref)
    groups = piece_ref.shape[0]
    piece = jnp.concatenate(
        [piece_ref[k] for k in range(1, FEAT_FIRST + 1)]
        + [piece_ref[0]]
        + [piece_ref[k] for k in range(FEAT_FIRST + 1, groups)],
        axis=0,
    )
    back = jnp.dot(weight_ref[...], piece, preferred_element_type=jnp.float32)
    back = back.astype(jnp.bfloat16)
    for b in range(block_count):
        back_ref[b] = back[:, b * LANES : (b + 1) * LANES]
    term = lax.dot_general(
        agg_ref[...], piece, (((1,), (1,)), ((), ())), preferred_element_type=jnp.float32
    )
    for k in range(wide):
        extra_ref[:, k, :] = term[:, k * LANES : (k + 1) * LANES]
    extra_ref[:, wide:, :] = jnp.zeros_like(extra_ref[:, wide:, :])
    for k in range(peers):
        value = number_ref[k].astype(jnp.float32)
        extra_ref[k, pl.ds(wide, 1), :] = jnp.full((1, LANES), value, jnp.float32)
    msg_ref[:, rows:, :] = extra_ref[:, :EXTRA, :].astype(jnp.bfloat16)
    for start in range(0, tile_total, GROUP):
        products, places = [], []
        for t in range(start, min(start + GROUP, tile_total)):
            products.append(
                jnp.dot(back_ref[dst_ref[t]], tiles_ref[t], preferred_element_type=jnp.float32)
            )
            places.append(place_ref[t])
        for place, product in zip(places, products):
            acc_ref[place] += product
    msg_ref[:, :rows, :] = acc_ref[:peers].astype(jnp.bfloat16)


def master_kernel(wide, got_ref, nodes_ref, msg_ref):
    peers = got_ref.shape[0]
    got_ref = got_ref.reshape(peers, got_ref.shape[1] * got_ref.shape[2], LANES)
    rows, columns = nodes_ref.shape
    block_count = columns // LANES
    msg_ref = msg_ref.reshape(peers, rows + wide, LANES)
    tail = got_ref[:, rows:, :].astype(jnp.float32)
    numbers = [tail[p, wide : wide + 1, :] for p in range(peers)]
    sums = [jnp.zeros((rows, LANES), jnp.float32) for _ in range(block_count)]
    for p in range(peers):
        part = got_ref[p, :rows, :].astype(jnp.float32)
        for b in range(block_count):
            sums[b] = sums[b] + jnp.where(numbers[p] == float(b), part, 0.0)
    for b in range(block_count):
        nodes_ref[:, b * LANES : (b + 1) * LANES] = sums[b].astype(jnp.bfloat16)
    for p in range(peers):
        pick = sums[0]
        for b in range(1, block_count):
            pick = jnp.where(numbers[p] == float(b), sums[b], pick)
        msg_ref[p, :rows, :] = pick.astype(jnp.bfloat16)
    total = jnp.sum(tail, axis=0)[:wide].astype(jnp.bfloat16)
    for p in range(peers):
        msg_ref[p, rows:, :] = total


def mirror_kernel(
    wide, peer_ref, got_ref, kept_ref, mirrors_hbm, wgrad_hbm, nodes_hbm,
    wgrad_ref, mirrors_ref, sems,
):
    peers = got_ref.shape[0]
    rows = wgrad_ref.shape[0]
    got_ref = got_ref.reshape(peers, rows + wide, LANES)
    moves = [pltpu.make_async_copy(kept_ref, nodes_hbm, sems.at[1])]
    moves[0].start()
    tail = got_ref[:, rows:, :].astype(jnp.float32)
    for k in range(wide):
        wgrad_ref[:, k * LANES : (k + 1) * LANES] = tail[:, k, :]
    moves.append(pltpu.make_async_copy(wgrad_ref, wgrad_hbm, sems.at[2]))
    moves[1].start()
    part = peers // 2
    for c in range(2):
        for s in range(c * part, (c + 1) * part):
            mirrors_ref[:, s * LANES : (s + 1) * LANES] = got_ref[peer_ref[s], :rows, :]
        span = pl.ds(c * part * LANES, part * LANES)
        move = pltpu.make_async_copy(mirrors_ref.at[:, span], mirrors_hbm.at[:, span], sems.at[3 + c])
        move.start()
        moves.append(move)
    for move in moves:
        move.wait()


def in_hbm(array):
    return pltpu.with_memory_space_constraint(array, pltpu.HBM)


def body(
    grad_out,
    saved_agg,
    weight,
    tile_values,
    tile_dst,
    tile_slot,
    tile_count,
    mirror_owner,
    mirror_local,
):
    rows, columns = grad_out.shape
    block_count = columns // LANES
    peers = mirror_owner.shape[1]
    features = weight.shape[1]
    wide = features // LANES
    groups = features // rows
    height = rows + EXTRA
    dom_groups = [order_of(DOM_FIRST, peers)]
    vmem = pl.BlockSpec(memory_space=pltpu.VMEM)
    smem = pl.BlockSpec(memory_space=pltpu.SMEM)
    hbm = pl.BlockSpec(memory_space=pltpu.HBM)
    params = pltpu.CompilerParams(vmem_limit_bytes=VMEM_BYTES)

    operands = (weight, saved_agg, tile_values)
    copies, dst, place, peer, number, *near = pl.pallas_call(
        stage_kernel,
        out_shape=(
            pltpu.VMEM((groups, rows, columns), grad_out.dtype),
            pltpu.SMEM(tile_dst.shape, jnp.int32),
            pltpu.SMEM(tile_slot.shape, jnp.int32),
            pltpu.SMEM((peers,), jnp.int32),
            pltpu.SMEM((peers,), jnp.int32),
            *(pltpu.VMEM(x.shape, x.dtype) for x in operands),
        ),
        in_specs=[hbm] * 3 + [smem] + [hbm] * 5,
        out_specs=(vmem,) + (smem,) * 4 + (vmem,) * 3,
        scratch_shapes=[
            pltpu.VMEM(grad_out.shape, grad_out.dtype),
            pltpu.SMEM(tile_slot.shape, jnp.int32),
            pltpu.SMEM(mirror_owner.shape, jnp.int32),
            pltpu.SMEM(mirror_local.shape, jnp.int32),
            pltpu.SemaphoreType.DMA((8,)),
        ],
        compiler_params=params,
        name="stage",
    )(
        *map(in_hbm, (grad_out, tile_dst, tile_slot)), tile_count,
        *map(in_hbm, (mirror_owner, mirror_local, *operands)),
    )
    with jax.named_scope("gather_features"):
        piece = lax.all_to_all(
            copies, "feat", 0, 0, tiled=True, axis_index_groups=[order_of(FEAT_FIRST, groups)]
        )
    message = pl.pallas_call(
        partial_kernel,
        out_shape=pltpu.VMEM((peers, height // 2, 2, LANES), jnp.bfloat16),
        in_specs=[smem] * 3 + [vmem] * 4,
        out_specs=vmem,
        scratch_shapes=[
            pltpu.VMEM((block_count, rows, LANES), jnp.bfloat16),
            pltpu.VMEM((peers + 1, rows, LANES), jnp.float32),
            pltpu.VMEM((peers, 8, LANES), jnp.float32),
        ],
        compiler_params=params,
        name="partials",
    )(dst, place, number, piece, *near)
    with jax.named_scope("to_masters"):
        got = lax.all_to_all(message, "dom", 0, 0, tiled=True, axis_index_groups=dom_groups)
    kept, answer = pl.pallas_call(
        functools.partial(master_kernel, wide),
        out_shape=(
            pltpu.VMEM((rows, columns), jnp.bfloat16),
            pltpu.VMEM((peers, (rows + wide) // wide, wide, LANES), jnp.bfloat16),
        ),
        in_specs=[vmem],
        out_specs=(vmem, vmem),
        compiler_params=params,
        name="masters",
    )(got)
    with jax.named_scope("to_mirrors"):
        back = lax.all_to_all(answer, "dom", 0, 0, tiled=True, axis_index_groups=dom_groups)
    grad_mirrors, weight_grad, grad_nodes = pl.pallas_call(
        functools.partial(mirror_kernel, wide),
        out_shape=(
            pltpu.HBM((rows, peers * LANES), jnp.bfloat16),
            pltpu.HBM((rows, features), jnp.float32),
            pltpu.HBM((rows, columns), jnp.bfloat16),
        ),
        in_specs=[smem, vmem, vmem],
        out_specs=(hbm, hbm, hbm),
        scratch_shapes=[
            pltpu.VMEM((rows, features), jnp.float32),
            pltpu.VMEM((rows, peers * LANES), jnp.bfloat16),
            pltpu.SemaphoreType.DMA((3 + 2,)),
        ],
        compiler_params=params,
        name="mirrors",
    )(peer, back, kept)
    return (grad_nodes, grad_mirrors, weight_grad)


def solution(mesh):
    in_specs = (
        P("feat", "dom"),
        P("feat", "dom"),
        P("feat", None),
        P("dom", None, None),
        P("dom"),
        P("dom"),
        P("dom"),
        P("dom", None),
        P("dom", None),
    )
    out_specs = (P("feat", "dom"), P("feat", "dom"), P("feat", None))
    return jax.shard_map(body, mesh=mesh, in_specs=in_specs, out_specs=out_specs, check_vma=False)
```

```python
import functools

import jax
import jax.numpy as jnp
from jax import lax
from jax.experimental import pallas as pl
from jax.experimental.pallas import tpu as pltpu
from jax.sharding import PartitionSpec as P

LANES = 128
GROUP = 48
EXTRA = 6
VMEM_BYTES = 16 * 1024 * 1024
DOM_FIRST = 19
FEAT_FIRST = 10


def order_of(first, count):
    return [first] + [k for k in range(count) if k != first]


def place_of(index, first):
    return jnp.where(index == first, 0, index + (index < first).astype(jnp.int32))


def stage_kernel(
    grad_hbm, dst_hbm, slot_hbm, count_ref, owner_hbm, local_hbm, weight_hbm, agg_hbm, tiles_hbm,
    copies_ref, dst_ref, place_ref, peer_ref, number_ref, weight_ref, agg_ref, tiles_ref,
    grad_ref, slot_ref, owner_ref, local_ref, sems,
):
    pairs = (
        (grad_hbm, grad_ref), (owner_hbm, owner_ref), (local_hbm, local_ref),
        (slot_hbm, slot_ref), (dst_hbm, dst_ref),
        (weight_hbm, weight_ref), (agg_hbm, agg_ref), (tiles_hbm, tiles_ref),
    )
    moves = [pltpu.make_async_copy(a, b, sems.at[k]) for k, (a, b) in enumerate(pairs)]
    for move in moves:
        move.start()
    peers = peer_ref.shape[0]
    tile_total = place_ref.shape[0]
    moves[0].wait()
    value = grad_ref[...]
    for k in range(copies_ref.shape[0]):
        copies_ref[k] = value
    moves[1].wait()
    moves[2].wait()

    def slot_step(s, carry):
        place = place_of(owner_ref[0, s], DOM_FIRST)
        peer_ref[s] = place
        number_ref[place] = local_ref[0, s]
        return carry

    lax.fori_loop(0, peers, slot_step, 0, unroll=8)
    moves[3].wait()
    count = count_ref[0]

    def tile_step(t, carry):
        place_ref[t] = jnp.where(t < count, peer_ref[slot_ref[t]], peers)
        return carry

    lax.fori_loop(0, tile_total, tile_step, 0, unroll=8)
    for move in moves[4:]:
        move.wait()


def partial_kernel(
    dst_ref, place_ref, number_ref, piece_ref, weight_ref, agg_ref, tiles_ref,
    msg_ref,
    back_ref, acc_ref, extra_ref,
):
    block_count, rows, _ = back_ref.shape
    peers = msg_ref.shape[0]
    msg_ref = msg_ref.reshape(peers, msg_ref.shape[1] * msg_ref.shape[2], LANES)
    tile_total = tiles_ref.shape[0]
    wide = weight_ref.shape[1] // LANES
    acc_ref[...] = jnp.zeros_like(acc_ref)
    groups = piece_ref.shape[0]
    piece = jnp.concatenate(
        [piece_ref[k] for k in range(1, FEAT_FIRST + 1)]
        + [piece_ref[0]]
        + [piece_ref[k] for k in range(FEAT_FIRST + 1, groups)],
        axis=0,
    )
    back = jnp.dot(weight_ref[...], piece, preferred_element_type=jnp.float32)
    back = back.astype(jnp.bfloat16)
    for b in range(block_count):
        back_ref[b] = back[:, b * LANES : (b + 1) * LANES]
    term = lax.dot_general(
        agg_ref[...], piece, (((1,), (1,)), ((), ())), preferred_element_type=jnp.float32
    )
    for k in range(wide):
        extra_ref[:, k, :] = term[:, k * LANES : (k + 1) * LANES]
    extra_ref[:, wide:, :] = jnp.zeros_like(extra_ref[:, wide:, :])
    for k in range(peers):
        value = number_ref[k].astype(jnp.float32)
        extra_ref[k, pl.ds(wide, 1), :] = jnp.full((1, LANES), value, jnp.float32)
    msg_ref[:, rows:, :] = extra_ref[:, :EXTRA, :].astype(jnp.bfloat16)
    for start in range(0, tile_total, GROUP):
        products, places = [], []
        for t in range(start, min(start + GROUP, tile_total)):
            products.append(
                jnp.dot(back_ref[dst_ref[t]], tiles_ref[t], preferred_element_type=jnp.float32)
            )
            places.append(place_ref[t])
        for place, product in zip(places, products):
            acc_ref[place] += product
    msg_ref[:, :rows, :] = acc_ref[:peers].astype(jnp.bfloat16)


def master_kernel(wide, got_ref, nodes_ref, msg_ref):
    peers = got_ref.shape[0]
    got_ref = got_ref.reshape(peers, got_ref.shape[1] * got_ref.shape[2], LANES)
    rows, columns = nodes_ref.shape
    block_count = columns // LANES
    msg_ref = msg_ref.reshape(peers, rows + wide, LANES)
    tail = got_ref[:, rows:, :].astype(jnp.float32)
    numbers = [jnp.broadcast_to(tail[p, wide : wide + 1, :], (rows, LANES)) for p in range(peers)]
    sums = [jnp.zeros((rows, LANES), jnp.float32) for _ in range(block_count)]
    for p in range(peers):
        part = got_ref[p, :rows, :].astype(jnp.float32)
        for b in range(block_count):
            sums[b] = sums[b] + jnp.where(numbers[p] == float(b), part, 0.0)
    for b in range(block_count):
        nodes_ref[:, b * LANES : (b + 1) * LANES] = sums[b].astype(jnp.bfloat16)
    for p in range(peers):
        pick = sums[0]
        for b in range(1, block_count):
            pick = jnp.where(numbers[p] == float(b), sums[b], pick)
        msg_ref[p, :rows, :] = pick.astype(jnp.bfloat16)
    total = jnp.sum(tail, axis=0)[:wide].astype(jnp.bfloat16)
    for p in range(peers):
        msg_ref[p, rows:, :] = total


def mirror_kernel(
    wide, peer_ref, got_ref, kept_ref, mirrors_hbm, wgrad_hbm, nodes_hbm,
    wgrad_ref, mirrors_ref, sems,
):
    peers = got_ref.shape[0]
    rows = wgrad_ref.shape[0]
    got_ref = got_ref.reshape(peers, rows + wide, LANES)
    moves = [pltpu.make_async_copy(kept_ref, nodes_hbm, sems.at[1])]
    moves[0].start()
    tail = got_ref[:, rows:, :].astype(jnp.float32)
    for k in range(wide):
        wgrad_ref[:, k * LANES : (k + 1) * LANES] = tail[:, k, :]
    moves.append(pltpu.make_async_copy(wgrad_ref, wgrad_hbm, sems.at[2]))
    moves[1].start()
    part = peers // 2
    for c in range(2):
        for s in range(c * part, (c + 1) * part):
            mirrors_ref[:, s * LANES : (s + 1) * LANES] = got_ref[peer_ref[s], :rows, :]
        span = pl.ds(c * part * LANES, part * LANES)
        move = pltpu.make_async_copy(mirrors_ref.at[:, span], mirrors_hbm.at[:, span], sems.at[3 + c])
        move.start()
        moves.append(move)
    for move in moves:
        move.wait()


def in_hbm(array):
    return pltpu.with_memory_space_constraint(array, pltpu.HBM)


def body(
    grad_out,
    saved_agg,
    weight,
    tile_values,
    tile_dst,
    tile_slot,
    tile_count,
    mirror_owner,
    mirror_local,
):
    rows, columns = grad_out.shape
    block_count = columns // LANES
    peers = mirror_owner.shape[1]
    features = weight.shape[1]
    wide = features // LANES
    groups = features // rows
    height = rows + EXTRA
    dom_groups = [order_of(DOM_FIRST, peers)]
    vmem = pl.BlockSpec(memory_space=pltpu.VMEM)
    smem = pl.BlockSpec(memory_space=pltpu.SMEM)
    hbm = pl.BlockSpec(memory_space=pltpu.HBM)
    params = pltpu.CompilerParams(vmem_limit_bytes=VMEM_BYTES)

    operands = (weight, saved_agg, tile_values)
    copies, dst, place, peer, number, *near = pl.pallas_call(
        stage_kernel,
        out_shape=(
            pltpu.VMEM((groups, rows, columns), grad_out.dtype),
            pltpu.SMEM(tile_dst.shape, jnp.int32),
            pltpu.SMEM(tile_slot.shape, jnp.int32),
            pltpu.SMEM((peers,), jnp.int32),
            pltpu.SMEM((peers,), jnp.int32),
            *(pltpu.VMEM(x.shape, x.dtype) for x in operands),
        ),
        in_specs=[hbm] * 3 + [smem] + [hbm] * 5,
        out_specs=(vmem,) + (smem,) * 4 + (vmem,) * 3,
        scratch_shapes=[
            pltpu.VMEM(grad_out.shape, grad_out.dtype),
            pltpu.SMEM(tile_slot.shape, jnp.int32),
            pltpu.SMEM(mirror_owner.shape, jnp.int32),
            pltpu.SMEM(mirror_local.shape, jnp.int32),
            pltpu.SemaphoreType.DMA((8,)),
        ],
        compiler_params=params,
        name="stage",
    )(
        *map(in_hbm, (grad_out, tile_dst, tile_slot)), tile_count,
        *map(in_hbm, (mirror_owner, mirror_local, *operands)),
    )
    with jax.named_scope("gather_features"):
        piece = lax.all_to_all(
            copies, "feat", 0, 0, tiled=True, axis_index_groups=[order_of(FEAT_FIRST, groups)]
        )
    message = pl.pallas_call(
        partial_kernel,
        out_shape=pltpu.VMEM((peers, height // 2, 2, LANES), jnp.bfloat16),
        in_specs=[smem] * 3 + [vmem] * 4,
        out_specs=vmem,
        scratch_shapes=[
            pltpu.VMEM((block_count, rows, LANES), jnp.bfloat16),
            pltpu.VMEM((peers + 1, rows, LANES), jnp.float32),
            pltpu.VMEM((peers, 8, LANES), jnp.float32),
        ],
        compiler_params=params,
        name="partials",
    )(dst, place, number, piece, *near)
    with jax.named_scope("to_masters"):
        got = lax.all_to_all(message, "dom", 0, 0, tiled=True, axis_index_groups=dom_groups)
    kept, answer = pl.pallas_call(
        functools.partial(master_kernel, wide),
        out_shape=(
            pltpu.VMEM((rows, columns), jnp.bfloat16),
            pltpu.VMEM((peers, (rows + wide) // wide, wide, LANES), jnp.bfloat16),
        ),
        in_specs=[vmem],
        out_specs=(vmem, vmem),
        compiler_params=params,
        name="masters",
    )(got)
    with jax.named_scope("to_mirrors"):
        back = lax.all_to_all(answer, "dom", 0, 0, tiled=True, axis_index_groups=dom_groups)
    grad_mirrors, weight_grad, grad_nodes = pl.pallas_call(
        functools.partial(mirror_kernel, wide),
        out_shape=(
            pltpu.HBM((rows, peers * LANES), jnp.bfloat16),
            pltpu.HBM((rows, features), jnp.float32),
            pltpu.HBM((rows, columns), jnp.bfloat16),
        ),
        in_specs=[smem, vmem, vmem],
        out_specs=(hbm, hbm, hbm),
        scratch_shapes=[
            pltpu.VMEM((rows, features), jnp.float32),
            pltpu.VMEM((rows, peers * LANES), jnp.bfloat16),
            pltpu.SemaphoreType.DMA((3 + 2,)),
        ],
        compiler_params=params,
        name="mirrors",
    )(peer, back, kept)
    return (grad_nodes, grad_mirrors, weight_grad)


def solution(mesh):
    in_specs = (
        P("feat", "dom"),
        P("feat", "dom"),
        P("feat", None),
        P("dom", None, None),
        P("dom"),
        P("dom"),
        P("dom"),
        P("dom", None),
        P("dom", None),
    )
    out_specs = (P("feat", "dom"), P("feat", "dom"), P("feat", None))
    return jax.shard_map(body, mesh=mesh, in_specs=in_specs, out_specs=out_specs, check_vma=False)
```

```python
import functools

import jax
import jax.numpy as jnp
from jax import lax
from jax.experimental import pallas as pl
from jax.experimental.pallas import tpu as pltpu
from jax.sharding import PartitionSpec as P

LANES = 128
GROUP = 48
EXTRA = 6
VMEM_BYTES = 16 * 1024 * 1024
DOM_FIRST = 19
FEAT_FIRST = 10


def order_of(first, count):
    return [first] + [k for k in range(count) if k != first]


def place_of(index, first):
    return jnp.where(index == first, 0, index + (index < first).astype(jnp.int32))


def stage_kernel(
    grad_hbm, dst_hbm, slot_hbm, count_ref, owner_hbm, local_hbm, weight_hbm, agg_hbm, tiles_hbm,
    copies_ref, dst_ref, place_ref, peer_ref, number_ref, weight_ref, agg_ref, tiles_ref,
    grad_ref, slot_ref, owner_ref, local_ref, sems,
):
    pairs = (
        (grad_hbm, grad_ref), (owner_hbm, owner_ref), (local_hbm, local_ref),
        (slot_hbm, slot_ref), (dst_hbm, dst_ref),
        (weight_hbm, weight_ref), (agg_hbm, agg_ref), (tiles_hbm, tiles_ref),
    )
    moves = [pltpu.make_async_copy(a, b, sems.at[k]) for k, (a, b) in enumerate(pairs)]
    for move in moves:
        move.start()
    peers = peer_ref.shape[0]
    tile_total = place_ref.shape[0]
    moves[0].wait()
    value = grad_ref[...]
    for k in range(copies_ref.shape[0]):
        copies_ref[k] = value
    moves[1].wait()
    moves[2].wait()

    def slot_step(s, carry):
        place = place_of(owner_ref[0, s], DOM_FIRST)
        peer_ref[s] = place
        number_ref[place] = local_ref[0, s]
        return carry

    lax.fori_loop(0, peers, slot_step, 0, unroll=8)
    moves[3].wait()
    count = count_ref[0]

    def tile_step(t, carry):
        place_ref[t] = jnp.where(t < count, peer_ref[slot_ref[t]], peers)
        return carry

    lax.fori_loop(0, tile_total, tile_step, 0, unroll=8)
    for move in moves[4:]:
        move.wait()


def partial_kernel(
    dst_ref, place_ref, number_ref, piece_ref, weight_ref, agg_ref, tiles_ref,
    msg_ref,
    back_ref, acc_ref, extra_ref,
):
    block_count, rows, _ = back_ref.shape
    peers = msg_ref.shape[0]
    msg_ref = msg_ref.reshape(peers, msg_ref.shape[1] * msg_ref.shape[2], LANES)
    tile_total = tiles_ref.shape[0]
    wide = weight_ref.shape[1] // LANES
    acc_ref[...] = jnp.zeros_like(acc_ref)
    groups = piece_ref.shape[0]
    piece = jnp.concatenate(
        [piece_ref[k] for k in range(1, FEAT_FIRST + 1)]
        + [piece_ref[0]]
        + [piece_ref[k] for k in range(FEAT_FIRST + 1, groups)],
        axis=0,
    )
    back = jnp.dot(weight_ref[...], piece, preferred_element_type=jnp.float32)
    back = back.astype(jnp.bfloat16)
    for b in range(block_count):
        back_ref[b] = back[:, b * LANES : (b + 1) * LANES]
    term = lax.dot_general(
        agg_ref[...], piece, (((1,), (1,)), ((), ())), preferred_element_type=jnp.float32
    )
    for k in range(wide):
        extra_ref[:, k, :] = term[:, k * LANES : (k + 1) * LANES]
    extra_ref[:, wide:, :] = jnp.zeros_like(extra_ref[:, wide:, :])
    for k in range(peers):
        value = number_ref[k].astype(jnp.float32)
        extra_ref[k, pl.ds(wide, 1), :] = jnp.full((1, LANES), value, jnp.float32)
    msg_ref[:, rows:, :] = extra_ref[:, :EXTRA, :].astype(jnp.bfloat16)
    for start in range(0, tile_total, GROUP):
        products, places = [], []
        for t in range(start, min(start + GROUP, tile_total)):
            products.append(
                jnp.dot(back_ref[dst_ref[t]], tiles_ref[t], preferred_element_type=jnp.float32)
            )
            places.append(place_ref[t])
        for place, product in zip(places, products):
            acc_ref[place] += product
    msg_ref[:, :rows, :] = acc_ref[:peers].astype(jnp.bfloat16)


def master_kernel(wide, got_ref, nodes_ref, msg_ref):
    peers = got_ref.shape[0]
    got_ref = got_ref.reshape(peers, got_ref.shape[1] * got_ref.shape[2], LANES)
    rows, columns = nodes_ref.shape
    block_count = columns // LANES
    msg_ref = msg_ref.reshape(peers, rows + wide, LANES)
    tail = got_ref[:, rows:, :].astype(jnp.float32)
    numbers = [jnp.broadcast_to(tail[p, wide : wide + 1, :], (rows, LANES)) for p in range(peers)]
    sums = [jnp.zeros((rows, LANES), jnp.float32) for _ in range(block_count)]
    for p in range(peers):
        part = got_ref[p, :rows, :].astype(jnp.float32)
        for b in range(block_count):
            sums[b] = sums[b] + jnp.where(numbers[p] == float(b), part, 0.0)
    for b in range(block_count):
        nodes_ref[:, b * LANES : (b + 1) * LANES] = sums[b].astype(jnp.bfloat16)
    for p in range(peers):
        pick = sums[0]
        for b in range(1, block_count):
            pick = jnp.where(numbers[p] == float(b), sums[b], pick)
        msg_ref[p, :rows, :] = pick.astype(jnp.bfloat16)
    total = jnp.sum(tail, axis=0)[:wide].astype(jnp.bfloat16)
    for p in range(peers):
        msg_ref[p, rows:, :] = total


def mirror_kernel(
    wide, peer_ref, got_ref, kept_ref, mirrors_hbm, wgrad_hbm, nodes_hbm,
    wgrad_ref, mirrors_ref, sems,
):
    peers = got_ref.shape[0]
    rows = wgrad_ref.shape[0]
    got_ref = got_ref.reshape(peers, rows + wide, LANES)
    moves = [pltpu.make_async_copy(kept_ref, nodes_hbm, sems.at[1])]
    moves[0].start()
    part = peers // 2
    for c in range(2):
        for s in range(c * part, (c + 1) * part):
            mirrors_ref[:, s * LANES : (s + 1) * LANES] = got_ref[peer_ref[s], :rows, :]
        span = pl.ds(c * part * LANES, part * LANES)
        move = pltpu.make_async_copy(mirrors_ref.at[:, span], mirrors_hbm.at[:, span], sems.at[3 + c])
        move.start()
        moves.append(move)
    tail = got_ref[:, rows:, :].astype(jnp.float32)
    for k in range(wide):
        wgrad_ref[:, k * LANES : (k + 1) * LANES] = tail[:, k, :]
    move = pltpu.make_async_copy(wgrad_ref, wgrad_hbm, sems.at[2])
    move.start()
    moves.append(move)
    for move in moves:
        move.wait()


def in_hbm(array):
    return pltpu.with_memory_space_constraint(array, pltpu.HBM)


def body(
    grad_out,
    saved_agg,
    weight,
    tile_values,
    tile_dst,
    tile_slot,
    tile_count,
    mirror_owner,
    mirror_local,
):
    rows, columns = grad_out.shape
    block_count = columns // LANES
    peers = mirror_owner.shape[1]
    features = weight.shape[1]
    wide = features // LANES
    groups = features // rows
    height = rows + EXTRA
    dom_groups = [order_of(DOM_FIRST, peers)]
    vmem = pl.BlockSpec(memory_space=pltpu.VMEM)
    smem = pl.BlockSpec(memory_space=pltpu.SMEM)
    hbm = pl.BlockSpec(memory_space=pltpu.HBM)
    params = pltpu.CompilerParams(vmem_limit_bytes=VMEM_BYTES)

    operands = (weight, saved_agg, tile_values)
    copies, dst, place, peer, number, *near = pl.pallas_call(
        stage_kernel,
        out_shape=(
            pltpu.VMEM((groups, rows, columns), grad_out.dtype),
            pltpu.SMEM(tile_dst.shape, jnp.int32),
            pltpu.SMEM(tile_slot.shape, jnp.int32),
            pltpu.SMEM((peers,), jnp.int32),
            pltpu.SMEM((peers,), jnp.int32),
            *(pltpu.VMEM(x.shape, x.dtype) for x in operands),
        ),
        in_specs=[hbm] * 3 + [smem] + [hbm] * 5,
        out_specs=(vmem,) + (smem,) * 4 + (vmem,) * 3,
        scratch_shapes=[
            pltpu.VMEM(grad_out.shape, grad_out.dtype),
            pltpu.SMEM(tile_slot.shape, jnp.int32),
            pltpu.SMEM(mirror_owner.shape, jnp.int32),
            pltpu.SMEM(mirror_local.shape, jnp.int32),
            pltpu.SemaphoreType.DMA((8,)),
        ],
        compiler_params=params,
        name="stage",
    )(
        *map(in_hbm, (grad_out, tile_dst, tile_slot)), tile_count,
        *map(in_hbm, (mirror_owner, mirror_local, *operands)),
    )
    with jax.named_scope("gather_features"):
        piece = lax.all_to_all(
            copies, "feat", 0, 0, tiled=True, axis_index_groups=[order_of(FEAT_FIRST, groups)]
        )
    message = pl.pallas_call(
        partial_kernel,
        out_shape=pltpu.VMEM((peers, height // 2, 2, LANES), jnp.bfloat16),
        in_specs=[smem] * 3 + [vmem] * 4,
        out_specs=vmem,
        scratch_shapes=[
            pltpu.VMEM((block_count, rows, LANES), jnp.bfloat16),
            pltpu.VMEM((peers + 1, rows, LANES), jnp.float32),
            pltpu.VMEM((peers, 8, LANES), jnp.float32),
        ],
        compiler_params=params,
        name="partials",
    )(dst, place, number, piece, *near)
    with jax.named_scope("to_masters"):
        got = lax.all_to_all(message, "dom", 0, 0, tiled=True, axis_index_groups=dom_groups)
    kept, answer = pl.pallas_call(
        functools.partial(master_kernel, wide),
        out_shape=(
            pltpu.VMEM((rows, columns), jnp.bfloat16),
            pltpu.VMEM((peers, (rows + wide) // wide, wide, LANES), jnp.bfloat16),
        ),
        in_specs=[vmem],
        out_specs=(vmem, vmem),
        compiler_params=params,
        name="masters",
    )(got)
    with jax.named_scope("to_mirrors"):
        back = lax.all_to_all(answer, "dom", 0, 0, tiled=True, axis_index_groups=dom_groups)
    grad_mirrors, weight_grad, grad_nodes = pl.pallas_call(
        functools.partial(mirror_kernel, wide),
        out_shape=(
            pltpu.HBM((rows, peers * LANES), jnp.bfloat16),
            pltpu.HBM((rows, features), jnp.float32),
            pltpu.HBM((rows, columns), jnp.bfloat16),
        ),
        in_specs=[smem, vmem, vmem],
        out_specs=(hbm, hbm, hbm),
        scratch_shapes=[
            pltpu.VMEM((rows, features), jnp.float32),
            pltpu.VMEM((rows, peers * LANES), jnp.bfloat16),
            pltpu.SemaphoreType.DMA((3 + 2,)),
        ],
        compiler_params=params,
        name="mirrors",
    )(peer, back, kept)
    return (grad_nodes, grad_mirrors, weight_grad)


def solution(mesh):
    in_specs = (
        P("feat", "dom"),
        P("feat", "dom"),
        P("feat", None),
        P("dom", None, None),
        P("dom"),
        P("dom"),
        P("dom"),
        P("dom", None),
        P("dom", None),
    )
    out_specs = (P("feat", "dom"), P("feat", "dom"), P("feat", None))
    return jax.shard_map(body, mesh=mesh, in_specs=in_specs, out_specs=out_specs, check_vma=False)
```

```python
import functools

import jax
import jax.numpy as jnp
from jax import lax
from jax.experimental import pallas as pl
from jax.experimental.pallas import tpu as pltpu
from jax.sharding import PartitionSpec as P

LANES = 128
GROUP = 48
EXTRA = 6
VMEM_BYTES = 16 * 1024 * 1024
DOM_FIRST = 19
FEAT_FIRST = 10


def order_of(first, count):
    return [first] + [k for k in range(count) if k != first]


def place_of(index, first):
    return jnp.where(index == first, 0, index + (index < first).astype(jnp.int32))


def stage_kernel(
    grad_hbm, dst_hbm, slot_hbm, count_ref, owner_hbm, local_hbm, weight_hbm, agg_hbm, tiles_hbm,
    copies_ref, dst_ref, place_ref, peer_ref, number_ref, weight_ref, agg_ref, tiles_ref,
    grad_ref, slot_ref, owner_ref, local_ref, sems,
):
    pairs = (
        (grad_hbm, grad_ref), (owner_hbm, owner_ref), (local_hbm, local_ref),
        (slot_hbm, slot_ref), (dst_hbm, dst_ref),
        (weight_hbm, weight_ref), (agg_hbm, agg_ref), (tiles_hbm, tiles_ref),
    )
    moves = [pltpu.make_async_copy(a, b, sems.at[k]) for k, (a, b) in enumerate(pairs)]
    for move in (moves[0], moves[-1], *moves[1:-1]):
        move.start()
    peers = peer_ref.shape[0]
    tile_total = place_ref.shape[0]
    moves[0].wait()
    value = grad_ref[...]
    for k in range(copies_ref.shape[0]):
        copies_ref[k] = value
    moves[1].wait()
    moves[2].wait()

    def slot_step(s, carry):
        place = place_of(owner_ref[0, s], DOM_FIRST)
        peer_ref[s] = place
        number_ref[place] = local_ref[0, s]
        return carry

    lax.fori_loop(0, peers, slot_step, 0, unroll=8)
    moves[3].wait()
    count = count_ref[0]

    def tile_step(t, carry):
        place_ref[t] = jnp.where(t < count, peer_ref[slot_ref[t]], peers)
        return carry

    lax.fori_loop(0, tile_total, tile_step, 0, unroll=8)
    for move in moves[4:]:
        move.wait()


def partial_kernel(
    dst_ref, place_ref, number_ref, piece_ref, weight_ref, agg_ref, tiles_ref,
    msg_ref,
    back_ref, acc_ref, extra_ref,
):
    block_count, rows, _ = back_ref.shape
    peers = msg_ref.shape[0]
    msg_ref = msg_ref.reshape(peers, msg_ref.shape[1] * msg_ref.shape[2], LANES)
    tile_total = tiles_ref.shape[0]
    wide = weight_ref.shape[1] // LANES
    acc_ref[...] = jnp.zeros_like(acc_ref)
    groups = piece_ref.shape[0]
    piece = jnp.concatenate(
        [piece_ref[k] for k in range(1, FEAT_FIRST + 1)]
        + [piece_ref[0]]
        + [piece_ref[k] for k in range(FEAT_FIRST + 1, groups)],
        axis=0,
    )
    back = jnp.dot(weight_ref[...], piece, preferred_element_type=jnp.float32)
    back = back.astype(jnp.bfloat16)
    for b in range(block_count):
        back_ref[b] = back[:, b * LANES : (b + 1) * LANES]
    term = lax.dot_general(
        agg_ref[...], piece, (((1,), (1,)), ((), ())), preferred_element_type=jnp.float32
    )
    for k in range(wide):
        extra_ref[:, k, :] = term[:, k * LANES : (k + 1) * LANES]
    extra_ref[:, wide:, :] = jnp.zeros_like(extra_ref[:, wide:, :])
    for k in range(peers):
        value = number_ref[k].astype(jnp.float32)
        extra_ref[k, pl.ds(wide, 1), :] = jnp.full((1, LANES), value, jnp.float32)
    msg_ref[:, rows:, :] = extra_ref[:, :EXTRA, :].astype(jnp.bfloat16)
    for start in range(0, tile_total, GROUP):
        products, places = [], []
        for t in range(start, min(start + GROUP, tile_total)):
            products.append(
                jnp.dot(back_ref[dst_ref[t]], tiles_ref[t], preferred_element_type=jnp.float32)
            )
            places.append(place_ref[t])
        for place, product in zip(places, products):
            acc_ref[place] += product
    msg_ref[:, :rows, :] = acc_ref[:peers].astype(jnp.bfloat16)


def master_kernel(wide, got_ref, nodes_ref, msg_ref):
    peers = got_ref.shape[0]
    got_ref = got_ref.reshape(peers, got_ref.shape[1] * got_ref.shape[2], LANES)
    rows, columns = nodes_ref.shape
    block_count = columns // LANES
    msg_ref = msg_ref.reshape(peers, rows + wide, LANES)
    tail = got_ref[:, rows:, :].astype(jnp.float32)
    numbers = [jnp.broadcast_to(tail[p, wide : wide + 1, :], (rows, LANES)) for p in range(peers)]
    sums = [jnp.zeros((rows, LANES), jnp.float32) for _ in range(block_count)]
    for p in range(peers):
        part = got_ref[p, :rows, :].astype(jnp.float32)
        for b in range(block_count):
            sums[b] = sums[b] + jnp.where(numbers[p] == float(b), part, 0.0)
    for b in range(block_count):
        nodes_ref[:, b * LANES : (b + 1) * LANES] = sums[b].astype(jnp.bfloat16)
    for p in range(peers):
        pick = sums[0]
        for b in range(1, block_count):
            pick = jnp.where(numbers[p] == float(b), sums[b], pick)
        msg_ref[p, :rows, :] = pick.astype(jnp.bfloat16)
    total = jnp.sum(tail, axis=0)[:wide].astype(jnp.bfloat16)
    for p in range(peers):
        msg_ref[p, rows:, :] = total


def mirror_kernel(
    wide, peer_ref, got_ref, kept_ref, mirrors_hbm, wgrad_hbm, nodes_hbm,
    wgrad_ref, mirrors_ref, sems,
):
    peers = got_ref.shape[0]
    rows = wgrad_ref.shape[0]
    got_ref = got_ref.reshape(peers, rows + wide, LANES)
    moves = [pltpu.make_async_copy(kept_ref, nodes_hbm, sems.at[1])]
    moves[0].start()
    part = peers // 2
    for c in range(2):
        for s in range(c * part, (c + 1) * part):
            mirrors_ref[:, s * LANES : (s + 1) * LANES] = got_ref[peer_ref[s], :rows, :]
        span = pl.ds(c * part * LANES, part * LANES)
        move = pltpu.make_async_copy(mirrors_ref.at[:, span], mirrors_hbm.at[:, span], sems.at[3 + c])
        move.start()
        moves.append(move)
    tail = got_ref[:, rows:, :].astype(jnp.float32)
    for k in range(wide):
        wgrad_ref[:, k * LANES : (k + 1) * LANES] = tail[:, k, :]
    move = pltpu.make_async_copy(wgrad_ref, wgrad_hbm, sems.at[2])
    move.start()
    moves.append(move)
    for move in moves:
        move.wait()


def in_hbm(array):
    return pltpu.with_memory_space_constraint(array, pltpu.HBM)


def body(
    grad_out,
    saved_agg,
    weight,
    tile_values,
    tile_dst,
    tile_slot,
    tile_count,
    mirror_owner,
    mirror_local,
):
    rows, columns = grad_out.shape
    block_count = columns // LANES
    peers = mirror_owner.shape[1]
    features = weight.shape[1]
    wide = features // LANES
    groups = features // rows
    height = rows + EXTRA
    dom_groups = [order_of(DOM_FIRST, peers)]
    vmem = pl.BlockSpec(memory_space=pltpu.VMEM)
    smem = pl.BlockSpec(memory_space=pltpu.SMEM)
    hbm = pl.BlockSpec(memory_space=pltpu.HBM)
    params = pltpu.CompilerParams(vmem_limit_bytes=VMEM_BYTES)

    operands = (weight, saved_agg, tile_values)
    copies, dst, place, peer, number, *near = pl.pallas_call(
        stage_kernel,
        out_shape=(
            pltpu.VMEM((groups, rows, columns), grad_out.dtype),
            pltpu.SMEM(tile_dst.shape, jnp.int32),
            pltpu.SMEM(tile_slot.shape, jnp.int32),
            pltpu.SMEM((peers,), jnp.int32),
            pltpu.SMEM((peers,), jnp.int32),
            *(pltpu.VMEM(x.shape, x.dtype) for x in operands),
        ),
        in_specs=[hbm] * 3 + [smem] + [hbm] * 5,
        out_specs=(vmem,) + (smem,) * 4 + (vmem,) * 3,
        scratch_shapes=[
            pltpu.VMEM(grad_out.shape, grad_out.dtype),
            pltpu.SMEM(tile_slot.shape, jnp.int32),
            pltpu.SMEM(mirror_owner.shape, jnp.int32),
            pltpu.SMEM(mirror_local.shape, jnp.int32),
            pltpu.SemaphoreType.DMA((8,)),
        ],
        compiler_params=params,
        name="stage",
    )(
        *map(in_hbm, (grad_out, tile_dst, tile_slot)), tile_count,
        *map(in_hbm, (mirror_owner, mirror_local, *operands)),
    )
    with jax.named_scope("gather_features"):
        piece = lax.all_to_all(
            copies, "feat", 0, 0, tiled=True, axis_index_groups=[order_of(FEAT_FIRST, groups)]
        )
    message = pl.pallas_call(
        partial_kernel,
        out_shape=pltpu.VMEM((peers, height // 2, 2, LANES), jnp.bfloat16),
        in_specs=[smem] * 3 + [vmem] * 4,
        out_specs=vmem,
        scratch_shapes=[
            pltpu.VMEM((block_count, rows, LANES), jnp.bfloat16),
            pltpu.VMEM((peers + 1, rows, LANES), jnp.float32),
            pltpu.VMEM((peers, 8, LANES), jnp.float32),
        ],
        compiler_params=params,
        name="partials",
    )(dst, place, number, piece, *near)
    with jax.named_scope("to_masters"):
        got = lax.all_to_all(message, "dom", 0, 0, tiled=True, axis_index_groups=dom_groups)
    kept, answer = pl.pallas_call(
        functools.partial(master_kernel, wide),
        out_shape=(
            pltpu.VMEM((rows, columns), jnp.bfloat16),
            pltpu.VMEM((peers, (rows + wide) // wide, wide, LANES), jnp.bfloat16),
        ),
        in_specs=[vmem],
        out_specs=(vmem, vmem),
        compiler_params=params,
        name="masters",
    )(got)
    with jax.named_scope("to_mirrors"):
        back = lax.all_to_all(answer, "dom", 0, 0, tiled=True, axis_index_groups=dom_groups)
    grad_mirrors, weight_grad, grad_nodes = pl.pallas_call(
        functools.partial(mirror_kernel, wide),
        out_shape=(
            pltpu.HBM((rows, peers * LANES), jnp.bfloat16),
            pltpu.HBM((rows, features), jnp.float32),
            pltpu.HBM((rows, columns), jnp.bfloat16),
        ),
        in_specs=[smem, vmem, vmem],
        out_specs=(hbm, hbm, hbm),
        scratch_shapes=[
            pltpu.VMEM((rows, features), jnp.float32),
            pltpu.VMEM((rows, peers * LANES), jnp.bfloat16),
            pltpu.SemaphoreType.DMA((3 + 2,)),
        ],
        compiler_params=params,
        name="mirrors",
    )(peer, back, kept)
    return (grad_nodes, grad_mirrors, weight_grad)


def solution(mesh):
    in_specs = (
        P("feat", "dom"),
        P("feat", "dom"),
        P("feat", None),
        P("dom", None, None),
        P("dom"),
        P("dom"),
        P("dom"),
        P("dom", None),
        P("dom", None),
    )
    out_specs = (P("feat", "dom"), P("feat", "dom"), P("feat", None))
    return jax.shard_map(body, mesh=mesh, in_specs=in_specs, out_specs=out_specs, check_vma=False)
```
